128 devices in a mesh: tower: 2 (over z_hi), grp: 2 (over core), seq: 32 (over y, x, z_lo).
Axes of the slice: x: 4, y: 4, z: 4 (z_hi: 2, z_lo: 2; z = z_hi * 2 + z_lo), core: 2. Of those that a mesh axis runs over, the one named last changes fastest.
Arguments:
- queries: bfloat16 [2, 8192, 3072], P('tower', 'seq', 'grp'), may hold values from -15 to 15, as said below
- keys: bfloat16 [2, 8192, 3072], P('tower', 'seq', 'grp'), may hold values from -6 to 6, as said below
- values: bfloat16 [2, 8192, 3072], P('tower', 'seq', 'grp'), may hold values from -6 to 6
- stamps: int32 [2, 8192], P('tower', 'seq'), may hold values from 0 to 8191, as said below
- partner: int32 [32], replicated, may hold values from 0 to 31, as said below
- w_out: bfloat16 [2, 3072, 3072], P('tower', 'grp'), may hold values from -0.109375 to 0.109375
Outputs:
- mixed_out: bfloat16 [2, 8192, 3072], P('tower', 'seq', 'grp')
The draws below stay inside these ranges and needn't reach their ends.
Inputs may be any that keep to these rules, and one draw needn't show every extreme that they name: queries are bounded as stated. keys are bounded as stated. Video frames are runs of 1560 consecutive video rows starting at multiples of 1560; every video token's stamp is the first row index of its frame, so a frame may span several shards. The audio tokens at shard position partner[s] carry the distinct stamps s * 256 to (s + 1) * 256 - 1. partner is a permutation of the 32 shard positions.
All inputs are finite; a program needn't handle non-finite values.
Results may differ from the reference program's by a relative error of at most 0.015.
Values may be sent and summed in bfloat16 or wider, within the bound.
A program may use at most 256 MiB of HBM per device.

```python
import math
import jax
import jax.numpy as jnp
from jax import lax

D = 3072
HEADS = 24
HEAD = 128
TOK_DEV = 256
TPF = 1560
LEN = 8192
N_SEQ = 32


def clock_table(key):
    shard_order = jax.random.permutation(jax.random.fold_in(key, 101), N_SEQ).astype(jnp.int32)
    rows = jnp.arange(LEN, dtype=jnp.int32)
    video_time = rows // TPF * TPF
    inverse = jnp.argsort(shard_order).astype(jnp.int32)
    audio_time = (inverse[:, None] * TOK_DEV + jnp.arange(TOK_DEV, dtype=jnp.int32)[None, :]).reshape(-1)
    return (shard_order, jnp.stack([video_time, audio_time]).astype(jnp.int32))


def draw_partner(key, part):
    shard_order, times = clock_table(key)
    return shard_order


def draw_stamps(key, part):
    shard_order, times = clock_table(key)
    return times


def draw_queries(key, part):
    key = jax.random.fold_in(key, 3)
    result = jnp.clip(2.5 * jax.random.normal(key, (2, LEN, D), jnp.float32), -15.0, 15.0)
    return result.astype(jnp.bfloat16)


def draw_keys(key, part):
    key = jax.random.fold_in(key, 4)
    result = jnp.clip(jax.random.normal(key, (2, LEN, D), jnp.float32), -6.0, 6.0)
    return result.astype(jnp.bfloat16)


def steps_of(own_key, shape, cuts, smallest, largest):
    factor_of = 1.0
    for axis_at, shards_of in cuts:
        draws = jax.random.uniform(jax.random.fold_in(jax.random.fold_in(own_key, 6), axis_at), (shards_of,), jnp.float32, smallest / len(cuts), largest / len(cuts))
        factor_of = factor_of * jnp.repeat(jnp.exp(draws), shape[axis_at] // shards_of).reshape((-1,) + (1,) * (len(shape) - 1 - axis_at))
    return factor_of


def gaussian(own_key, dims, deviation, most, cuts=(), kind=jnp.bfloat16):
    values = jax.random.normal(own_key, dims, jnp.float32) * deviation
    if len(cuts) > 0:
        values = steps_of(own_key, dims, cuts, -0.22, 0.18) * values
    return jnp.clip(values, min=-most, max=most).astype(kind)


def setup_inputs(seed: int = 0) -> dict:
    streams_of = jax.random.split(jax.random.key(seed), 7)
    queries = draw_queries(jax.random.fold_in(streams_of[6], 71), 0)
    keys = draw_keys(jax.random.fold_in(streams_of[6], 71), 0)
    values = gaussian(streams_of[2], (2, LEN, D), 1.0, 6.0, ((0, 2), (1, 32), (2, 2)))
    stamps = draw_stamps(jax.random.fold_in(streams_of[6], 71), 0)
    partner = draw_partner(jax.random.fold_in(streams_of[6], 71), 0)
    w_out = gaussian(streams_of[5], (2, D, D), D ** -0.5, 0.109375, ((0, 2), (1, 2)))
    return dict(queries=queries, keys=keys, values=values, stamps=stamps, partner=partner, w_out=w_out)


def rotate(inputs, times):
    row_count = inputs.shape[0]
    half_size = HEAD // 2
    frequency = jnp.exp(-math.log(10000.0) * jnp.arange(half_size, dtype=jnp.float32) / half_size)
    angles = times.astype(jnp.float32)[:, None] * frequency[None, :]
    cosine = jnp.cos(angles)[:, None, :]
    sine_part = jnp.sin(angles)[:, None, :]
    halves = inputs.astype(jnp.float32).reshape(row_count, -1, 2, half_size)
    first_half = halves[:, :, 0]
    second_half = halves[:, :, 1]
    turned = jnp.stack([first_half * cosine - second_half * sine_part, first_half * sine_part + second_half * cosine], axis=2)
    return turned.reshape(row_count, -1).astype(jnp.bfloat16)

def attend(query_block, key_block, value_block):
    row_count = query_block.shape[0]
    query_heads = query_block.astype(jnp.float32).reshape(row_count, HEADS, HEAD)
    key_heads = key_block.astype(jnp.float32).reshape(key_block.shape[0], HEADS, HEAD)
    value_heads = value_block.astype(jnp.float32).reshape(value_block.shape[0], HEADS, HEAD)
    scores = jnp.einsum('qhd,khd->hqk', query_heads, key_heads) * (1.0 / math.sqrt(HEAD))
    row_max = lax.optimization_barrier(jnp.max(scores, axis=-1, keepdims=True))
    exponent = jnp.exp(scores - row_max)
    totals = lax.optimization_barrier(jnp.sum(exponent, axis=-1))
    weights = lax.optimization_barrier(exponent.astype(jnp.bfloat16)).astype(jnp.float32)
    numerator = jnp.einsum('hqk,khd->hqd', weights, value_heads)
    result = numerator / totals[:, :, None]
    return jnp.transpose(result, (1, 0, 2)).reshape(row_count, -1)

def reference(queries, keys, values, stamps, partner, w_out):
    shards = jnp.arange(N_SEQ, dtype=jnp.int32)
    inverse = lax.optimization_barrier(jnp.sum(jnp.where(partner[None, :] == shards[:, None], shards[None, :], 0), axis=1)).astype(jnp.int32)
    results = []
    for tower_id in range(2):
        other_id = 1 - tower_id
        own_queries = rotate(queries[tower_id], stamps[tower_id])
        own_keys = rotate(keys[tower_id], stamps[tower_id])
        own_values = values[tower_id]
        other_keys = rotate(keys[other_id], stamps[other_id])
        other_values = values[other_id]
        cross_of = partner if tower_id == 0 else inverse

        def shard_block(block_args):
            query_block, shard = block_args
            self_out = attend(query_block, own_keys, own_values)
            first_row = (cross_of[shard] * TOK_DEV).astype(jnp.int32)
            cross_keys = lax.dynamic_slice_in_dim(other_keys, first_row, TOK_DEV, 0)
            cross_values = lax.dynamic_slice_in_dim(other_values, first_row, TOK_DEV, 0)
            cross_out = attend(query_block, cross_keys, cross_values)
            return (self_out + cross_out).astype(jnp.bfloat16)
        combined = lax.map(shard_block, (own_queries.reshape(N_SEQ, TOK_DEV, D), shards)).reshape(LEN, D)
        results.append(jnp.dot(combined, w_out[tower_id], preferred_element_type=jnp.float32).astype(jnp.bfloat16))
    return jnp.stack(results)
```

```python
import functools
import math

import jax
import jax.numpy as jnp
from jax import lax
from jax.experimental import pallas as pl
from jax.experimental.pallas import tpu as pltpu
from jax.sharding import PartitionSpec as P

HEAD = 128
TOK = 256
PHASES = 3
BLOCKS = 32
ROWS = 4 * TOK
MODEL = 3072
HALF = MODEL // 2
TILE = 512
SCALE = 1.0 / (math.sqrt(HEAD) * math.log(2.0))
F32 = jnp.float32
BF16 = jnp.bfloat16
MESH = pl.DeviceIdType.MESH

ALONG_X = (False, True, False)

ORDER = (
    (0, 0), (1, 0), (0, 1), (2, 0), (0, 2), (0, 3),
    (1, 1), (1, 2), (1, 3), (2, 1), (2, 2), (2, 3),
)
AHEAD = {
    ("below", 1): 8, ("above", 1): 8,
    ("below", 2): 16, ("above", 2): 16,
    ("cross", 0): 11, ("finish", 0): 15, ("project", 0): 18,
    ("cross", 1): 17, ("finish", 1): 21, ("project", 1): 22,
}
NEEDS = {
    (0, 0): ("own",), (0, 1): ("sib0",),
    (1, 0): ("below",), (1, 1): ("above",),
    (2, 0): ("sib1",), (2, 1): ("sib2",),
    (3, 0): ("opposite",), (3, 1): ("sib3",),
}


def plan():
    steps = [(phase, part, half) for phase, part in ORDER for half in range(2)]
    at = {}
    for place, (phase, part, half) in enumerate(steps):
        for event in NEEDS[(part, half)]:
            at[(event, phase)] = max(place - 1, -1)
            if event == "own":
                at[("ask", phase)] = max(place - 1, -1)
    at[("cross", 2)] = at[("sib3", 2)]
    for key, place in AHEAD.items():
        at[key] = place if key not in at else min(place, at[key])
    rank = ["ask", "own", "below", "above", "opposite", "sib0", "sib1", "sib2", "sib3",
            "cross", "finish", "project"]
    slots = {}
    for (event, phase), place in sorted(at.items(), key=lambda e: (e[1], rank.index(e[0][0]), e[0][1])):
        slots.setdefault(place, []).append((event, phase))
    return slots


def pick(index, values):
    chosen = jnp.int32(values[0])
    for place in range(1, len(values)):
        chosen = jnp.where(index == place, jnp.int32(values[place]), chosen)
    return chosen


def kernel(
    q_hbm, k_hbm, v_hbm, cos_ref, sin_ref, chosen_ref, w_hbm, out_ref,
    q_raw, k_raw, v_raw, w_ref, q_stage, kv_stage, kv, q_here, q_far, cross_mine, cross_far,
    picked, joined, home, total, part_out, part_in,
    acc, top, block_top, scores, weights,
    load_sem, kv_s, kv_r, q_s, q_r, line_s, line_r, opp_s, opp_r, sib_s, sib_r,
    far_s, far_r, cross_s, cross_r, home_s, home_r, part_s, part_r,
):
    t = lax.axis_index("tower")
    c = lax.axis_index("grp")
    s = lax.axis_index("seq")
    y, x, zl = s // 8, (s // 2) % 4, s % 2
    p = zl + t - 2 * zl * t

    def place(along_x, u, w, z):
        return w * 8 + u * 2 + z if along_x else u * 8 + w * 2 + z

    class Line:
        def __init__(self, along_x):
            self.along_x = along_x
            self.u, self.w = (x, y) if along_x else (y, x)
            self.a, self.wl = self.w // 2, self.w % 2
            self.r = self.wl * 2 + zl
            self.gl = self.wl * 2 + p
            self.i = 2 * self.w + zl
            self.mine = c == self.a

        def peer(self, r):
            return (t, self.a, place(self.along_x, self.u, 2 * c + r // 2, r % 2))

        def next(self, step):
            return (t, c, place(self.along_x, (self.u + step) % 4, self.w, zl))

        def chunk(self, step, core):
            return ((self.u + step) % 4) * 8 + 4 * core

    lines = {False: Line(False), True: Line(True)}
    sibling = (t, 1 - c, s)
    far = (1 - t, c, s + 1 - 2 * zl)

    def remote(src, dst, send, recv, device):
        return pltpu.make_async_remote_copy(
            src_ref=src, dst_ref=dst, send_sem=send, recv_sem=recv,
            device_id=device, device_id_type=MESH,
        )

    loads = [
        pltpu.make_async_copy(k_hbm.at[0], k_raw, load_sem.at[0]),
        pltpu.make_async_copy(v_hbm.at[0], v_raw, load_sem.at[1]),
        pltpu.make_async_copy(q_hbm.at[0], q_raw, load_sem.at[2]),
        pltpu.make_async_copy(w_hbm.at[0], w_ref, load_sem.at[3]),
    ]
    for load in loads:
        load.start()

    barrier = pltpu.get_barrier_semaphore()

    def greet(device):
        pl.semaphore_signal(barrier, inc=1, device_id=device, device_id_type=MESH)

    count = jnp.int32(6)
    for line in lines.values():
        for r in range(4):
            @pl.when(jnp.logical_not(jnp.logical_and(line.mine, line.r == r)))
            def _():
                greet(line.peer(r))
        greet(line.next(1))
        greet(line.next(3))
        count = count + 4 - jnp.where(line.mine, 1, 0)
    greet(sibling)
    greet(far)

    def turned(raw, head):
        entries = raw[:, pl.ds(pl.multiple_of(head * HEAD, HEAD), HEAD)].astype(F32)
        swapped = pltpu.roll(entries, HEAD // 2, 1)
        return (entries * cos_ref[...] + swapped * sin_ref[...]).astype(BF16)

    def deliver(phase, gl, src, dst, send, recv):
        line = lines[ALONG_X[phase]]
        r = (gl // 2) * 2 + (gl % 2 + t - 2 * (gl % 2) * t)
        here = jnp.logical_and(line.mine, line.r == r)

        @pl.when(here)
        def _():
            pltpu.make_async_copy(src, dst, recv).start()

        @pl.when(jnp.logical_not(here))
        def _():
            remote(src, dst, send, recv, line.peer(r)).start()

    def prepare_kv(phase):
        line = lines[ALONG_X[phase]]

        def one(gl, _):
            head = gl * PHASES + phase
            kv_stage[phase * 4 + gl, 0] = turned(k_raw, head)
            kv_stage[phase * 4 + gl, 1] = v_raw[:, pl.ds(pl.multiple_of(head * HEAD, HEAD), HEAD)]
            return 0

        lax.fori_loop(0, 4, one, 0)

    def send_kv(phase):
        line = lines[ALONG_X[phase]]
        for gl in range(4):
            deliver(phase, gl, kv_stage.at[phase * 4 + gl],
                    kv.at[phase * BLOCKS + line.u * 8 + line.i],
                    kv_s.at[phase * 4 + gl], kv_r.at[phase * 4 + line.r])

    def send_q(phase):
        line = lines[ALONG_X[phase]]

        def one(gl, _):
            q_stage[phase * 4 + gl] = turned(q_raw, gl * PHASES + phase)
            return 0

        lax.fori_loop(0, 4, one, 0)
        for gl in range(4):
            deliver(phase, gl, q_stage.at[phase * 4 + gl], q_here.at[phase * 4 + line.r],
                    q_s.at[phase * 4 + gl], q_r.at[phase * 4 + line.r])

    loads[0].wait()
    loads[1].wait()
    prepare_kv(0)
    pl.semaphore_wait(barrier, count)
    send_kv(0)
    loads[2].wait()
    send_q(0)
    prepare_kv(1)
    send_kv(1)
    send_q(1)
    prepare_kv(2)
    send_kv(2)
    send_q(2)

    acc[...] = jnp.zeros(acc.shape, F32)
    top[...] = jnp.full(top.shape, -1e30, F32)

    def blocks(phase, first, size):
        return kv.at[pl.ds(phase * BLOCKS + first, size)]

    def landed(dst, recv):
        remote(dst, dst, recv, recv, sibling).wait_recv()

    def to_sibling(phase, number, part):
        remote(part, part, sib_s.at[phase * 4 + number], sib_r.at[phase * 4 + number], sibling).start()

    def event(name, phase):
        line = lines[ALONG_X[phase]]
        if name == "ask":
            for r in range(4):
                landed(q_here.at[phase * 4 + r], q_r.at[phase * 4 + r])
            remote(q_here.at[pl.ds(phase * 4, 4)], q_far.at[pl.ds(phase * 4, 4)],
                   far_s.at[phase], far_r.at[phase], far).start()
        elif name == "own":
            first = line.chunk(0, c)
            for r in range(4):
                landed(kv.at[phase * BLOCKS + first + r], kv_r.at[phase * 4 + r])
            part = blocks(phase, first, 4)
            remote(part, part, line_s.at[phase * 2], line_r.at[phase * 2], line.next(1)).start()
            remote(part, part, line_s.at[phase * 2 + 1], line_r.at[phase * 2 + 1], line.next(3)).start()
            to_sibling(phase, 0, part)
        elif name == "below":
            first = line.chunk(3, c)
            part = blocks(phase, first, 4)
            landed(part, line_r.at[phase * 2])
            passed = blocks(phase, first, 2)
            remote(passed, passed, opp_s.at[phase * 2], opp_r.at[phase * 2], line.next(1)).start()
            to_sibling(phase, 1, part)
        elif name == "above":
            first = line.chunk(1, c)
            part = blocks(phase, first, 4)
            landed(part, line_r.at[phase * 2 + 1])
            passed = blocks(phase, first + 2, 2)
            remote(passed, passed, opp_s.at[phase * 2 + 1], opp_r.at[phase * 2 + 1], line.next(3)).start()
            to_sibling(phase, 2, part)
        elif name == "opposite":
            first = line.chunk(2, c)
            landed(blocks(phase, first, 2), opp_r.at[phase * 2])
            landed(blocks(phase, first + 2, 2), opp_r.at[phase * 2 + 1])
            to_sibling(phase, 3, blocks(phase, first, 4))
        elif name[:3] == "sib":
            number = int(name[3])
            step = (0, 3, 1, 2)[number]
            landed(blocks(phase, line.chunk(step, 1 - c), 4), sib_r.at[phase * 4 + number])
        elif name == "cross":
            cross(phase)
        elif name == "finish":
            finish(phase)
        else:
            project(phase)

    def cross(phase):
        kind = 4 if ALONG_X[phase] else 0
        want = [chosen_ref[kind + r] for r in range(4)]

        def select(step, _):
            rows = pl.ds(pl.multiple_of((step % 8) * 32, 32), 32)
            which = step // 8
            found = [jnp.zeros((32, HEAD), BF16) for r in range(4)]
            for block in range(BLOCKS):
                entries = kv[phase * BLOCKS + block, which, rows, :]
                for r in range(4):
                    found[r] = jnp.where(want[r] == block, entries, found[r])
            for r in range(4):
                picked[r, which, rows, :] = found[r]
            return 0

        lax.fori_loop(0, 16, select, 0)
        landed(q_far.at[pl.ds(phase * 4, 4)], far_r.at[phase])

        def one(r, _):
            found = lax.dot_general(
                q_far[phase * 4 + r], picked[r, 0], (((1,), (1,)), ((), ())),
                preferred_element_type=F32,
            ) * SCALE
            exponent = jnp.exp2(found - jnp.max(found, axis=1, keepdims=True))
            denominator = jnp.sum(exponent, axis=1, keepdims=True)
            numerator = jnp.dot(exponent.astype(BF16), picked[r, 1], preferred_element_type=F32)
            cross_mine[phase * 4 + r] = (numerator / denominator).astype(BF16)
            return 0

        lax.fori_loop(0, 4, one, 0)
        remote(cross_mine.at[pl.ds(phase * 4, 4)], cross_far.at[pl.ds(phase * 4, 4)],
               cross_s.at[phase], cross_r.at[phase], far).start()

    def finish(phase):
        line = lines[ALONG_X[phase]]
        landed(cross_far.at[pl.ds(phase * 4, 4)], cross_r.at[phase])
        for r in range(4):
            rows = pl.ds(phase * ROWS + r * TOK, TOK)
            own = acc[rows, 0:HEAD] / acc[rows, HEAD:]
            joined[phase * 4 + r] = (own + cross_far[phase * 4 + r].astype(F32)).astype(BF16)
            here = jnp.logical_and(line.mine, line.r == r)
            src, dst = joined.at[phase * 4 + r], home.at[phase * 4 + line.gl]
            recv = home_r.at[phase * 4 + line.gl]

            @pl.when(here)
            def _():
                pltpu.make_async_copy(src, dst, recv).start()

            @pl.when(jnp.logical_not(here))
            def _():
                remote(src, dst, home_s.at[phase * 4 + r], recv, line.peer(r)).start()

    def product(phase, columns):
        left = jnp.concatenate([home[phase * 4 + gl] for gl in range(4)], axis=1)
        right = jnp.concatenate(
            [w_ref[(gl * PHASES + phase) * HEAD:(gl * PHASES + phase + 1) * HEAD, columns]
             for gl in range(4)], axis=0)
        return jnp.dot(left, right, preferred_element_type=F32)

    def home_landed(phase):
        for gl in range(4):
            landed(home.at[phase * 4 + gl], home_r.at[phase * 4 + gl])

    def project(phase):
        home_landed(phase)
        if phase == 0:
            loads[3].wait()

        def one(n, _):
            columns = pl.ds(pl.multiple_of(n * TILE, TILE), TILE)
            value = product(phase, columns)
            total[:, columns] = value if phase == 0 else total[:, columns] + value
            return 0

        lax.fori_loop(0, MODEL // TILE, one, 0)

    def qk(phase, first, slot):
        rows = pl.ds(pl.multiple_of(phase * 4, 4), 4)
        queries = q_here[rows].reshape(ROWS, HEAD)
        keys = kv[pl.ds(phase * BLOCKS + first, 4), 0].reshape(ROWS, HEAD)
        found = lax.dot_general(
            queries, keys, (((1,), (1,)), ((), ())), preferred_element_type=F32
        )
        scores[slot] = found
        most = found[:, 0:HEAD]
        for column in range(1, ROWS // HEAD):
            most = jnp.maximum(most, found[:, column * HEAD:(column + 1) * HEAD])
        block_top[slot] = jnp.broadcast_to(
            jnp.max(most, axis=1, keepdims=True) * SCALE, (ROWS, HEAD)
        )

    def absorb(phase, first, slot):
        rows = pl.ds(pl.multiple_of(phase * ROWS, ROWS), ROWS)
        old_top = top[rows, :]
        new_top = jnp.maximum(old_top, block_top[slot])
        top[rows, :] = new_top
        for column in range(ROWS // HEAD):
            columns = slice(column * HEAD, (column + 1) * HEAD)
            weights[slot, :, columns] = jnp.exp2(
                scores[slot, :, columns] * SCALE - new_top
            ).astype(BF16)
        values = kv[pl.ds(phase * BLOCKS + first, 4), 1].reshape(ROWS, HEAD)
        widened = jnp.concatenate([values, jnp.ones_like(values)], axis=1)
        added = jnp.dot(weights[slot], widened, preferred_element_type=F32)
        rescale = jnp.exp2(old_top - new_top)
        acc[rows, :] = acc[rows, :] * jnp.concatenate([rescale, rescale], axis=1) + added

    def where_is(phase, part, half):
        u = jnp.where(pick(phase, [int(f) for f in ALONG_X]) == 1, x, y)
        step = jnp.where(part == 0, 0, jnp.where(part == 3, 2, 1 if half else 3))
        other = 1 - c
        split = other if half else c
        core = jnp.where(part == 1, c, jnp.where(part == 2, other, split))
        return ((u + step) % 4) * 8 + 4 * core

    slots = plan()
    phases = [phase for phase, part in ORDER]
    parts = [part for phase, part in ORDER]

    def events_of(pair, half):
        for number in range(len(ORDER)):
            todo = slots.get(2 * number + half, [])
            if todo:
                @pl.when(pair == number)
                def _(todo=todo):
                    for name, phase in todo:
                        event(name, phase)

    for name, phase in slots.get(-1, []):
        event(name, phase)
    qk(phases[0], where_is(jnp.int32(phases[0]), jnp.int32(parts[0]), 0), 0)

    def pair_step(pair, _):
        following = jnp.minimum(pair + 1, len(ORDER) - 1)
        phase, part = pick(pair, phases), pick(pair, parts)
        later_phase, later_part = pick(following, phases), pick(following, parts)
        events_of(pair, 0)
        qk(phase, where_is(phase, part, 1), 1)
        absorb(phase, where_is(phase, part, 0), 0)
        events_of(pair, 1)
        qk(later_phase, where_is(later_phase, later_part, 0), 0)
        absorb(phase, where_is(phase, part, 1), 1)
        return 0

    lax.fori_loop(0, len(ORDER), pair_step, 0)

    finish(2)
    home_landed(2)
    theirs, ours = (1 - c) * HALF, c * HALF

    def for_sibling(n, _):
        columns = pl.ds(pl.multiple_of(theirs + n * TILE, TILE), TILE)
        here = pl.ds(pl.multiple_of(n * TILE, TILE), TILE)
        part_out[:, here] = (total[:, columns] + product(2, columns)).astype(BF16)
        return 0

    lax.fori_loop(0, HALF // TILE, for_sibling, 0)
    exchange = remote(part_out, part_in, part_s, part_r, sibling)
    exchange.start()

    def for_us(n, _):
        columns = pl.ds(pl.multiple_of(ours + n * TILE, TILE), TILE)
        total[:, columns] = total[:, columns] + product(2, columns)
        return 0

    lax.fori_loop(0, HALF // TILE, for_us, 0)
    exchange.wait()

    def emit(n, _):
        columns = pl.ds(pl.multiple_of(ours + n * TILE, TILE), TILE)
        here = pl.ds(pl.multiple_of(n * TILE, TILE), TILE)
        out_ref[0, :, here] = (total[:, columns] + part_in[:, here].astype(F32)).astype(BF16)
        return 0

    lax.fori_loop(0, HALF // TILE, emit, 0)

    def sent(src, send):
        remote(src, src, send, send, sibling).wait_send()

    for phase in range(PHASES):
        line = lines[ALONG_X[phase]]
        for number in range(4):
            r = (number // 2) * 2 + (number % 2 + t - 2 * (number % 2) * t)

            @pl.when(jnp.logical_not(jnp.logical_and(line.mine, line.r == r)))
            def _():
                sent(kv_stage.at[phase * 4 + number], kv_s.at[phase * 4 + number])
                sent(q_stage.at[phase * 4 + number], q_s.at[phase * 4 + number])

            @pl.when(jnp.logical_not(jnp.logical_and(line.mine, line.r == number)))
            def _():
                sent(joined.at[phase * 4 + number], home_s.at[phase * 4 + number])

            sent(blocks(phase, 0, 4), sib_s.at[phase * 4 + number])
        for number in range(2):
            sent(blocks(phase, 0, 4), line_s.at[phase * 2 + number])
            sent(blocks(phase, 0, 2), opp_s.at[phase * 2 + number])
        sent(q_here.at[pl.ds(phase * 4, 4)], far_s.at[phase])
        sent(cross_mine.at[pl.ds(phase * 4, 4)], cross_s.at[phase])


def attention(queries, keys, values, cosine, sine, chosen, w_out):
    dma = pltpu.SemaphoreType.DMA
    anywhere = pl.BlockSpec(memory_space=pl.ANY)
    vmem = pl.BlockSpec(memory_space=pltpu.VMEM)
    heads = 4 * PHASES
    per_head = pltpu.VMEM((heads, TOK, HEAD), BF16)
    return pl.pallas_call(
        kernel,
        out_shape=jax.ShapeDtypeStruct((1, TOK, HALF), BF16),
        in_specs=[anywhere, anywhere, anywhere, vmem, vmem,
                  pl.BlockSpec(memory_space=pltpu.SMEM), anywhere],
        out_specs=vmem,
        scratch_shapes=[
            pltpu.VMEM((TOK, HALF), BF16),
            pltpu.VMEM((TOK, HALF), BF16),
            pltpu.VMEM((TOK, HALF), BF16),
            pltpu.VMEM((HALF, MODEL), BF16),
            per_head,
            pltpu.VMEM((heads, 2, TOK, HEAD), BF16),
            pltpu.VMEM((PHASES * BLOCKS, 2, TOK, HEAD), BF16),
            per_head, per_head, per_head, per_head,
            pltpu.VMEM((4, 2, TOK, HEAD), BF16),
            per_head, per_head,
            pltpu.VMEM((TOK, MODEL), F32),
            pltpu.VMEM((TOK, HALF), BF16),
            pltpu.VMEM((TOK, HALF), BF16),
            pltpu.VMEM((PHASES * ROWS, 2 * HEAD), F32),
            pltpu.VMEM((PHASES * ROWS, HEAD), F32),
            pltpu.VMEM((2, ROWS, HEAD), F32),
            pltpu.VMEM((2, ROWS, ROWS), F32),
            pltpu.VMEM((2, ROWS, ROWS), BF16),
            dma((4,)),
            dma((heads,)), dma((heads,)), dma((heads,)), dma((heads,)),
            dma((6,)), dma((6,)), dma((6,)), dma((6,)),
            dma((heads,)), dma((heads,)),
            dma((3,)), dma((3,)), dma((3,)), dma((3,)),
            dma((heads,)), dma((heads,)),
            dma, dma,
        ],
        compiler_params=pltpu.CompilerParams(
            collective_id=0, has_side_effects=True, vmem_limit_bytes=63 * 2**20
        ),
    )(queries, keys, values, cosine, sine, chosen, w_out)


def body(queries, keys, values, stamps, partner, w_out):
    half_size = HEAD // 2
    frequency = jnp.exp(-math.log(10000.0) * jnp.arange(half_size, dtype=F32) / half_size)
    angles = stamps[0].astype(F32)[:, None] * frequency[None, :]
    cosine, sine = jnp.cos(angles), jnp.sin(angles)
    cosine = jnp.concatenate([cosine, cosine], axis=1)
    sine = jnp.concatenate([-sine, sine], axis=1)
    t, c, s = lax.axis_index("tower"), lax.axis_index("grp"), lax.axis_index("seq")
    y, x = s // 8, (s // 2) % 4
    r = jnp.arange(4, dtype=jnp.int32)
    w, z = 2 * c + r // 2, r % 2
    asked = jnp.concatenate([y * 8 + w * 2 + z, w * 8 + x * 2 + z])
    shards = jnp.arange(BLOCKS, dtype=jnp.int32)[None, :]
    given = partner[None, :]
    forward = jnp.sum(jnp.where(shards == asked[:, None], given, 0), axis=1)
    inverse = jnp.sum(jnp.where(given == asked[:, None], shards, 0), axis=1)
    chosen = jnp.where(t == 1, forward, inverse)
    swapped = ((chosen // 2) % 4) * 8 + (chosen // 8) * 2 + chosen % 2
    chosen = jnp.where(jnp.arange(8) < 4, chosen, swapped).astype(jnp.int32)
    return attention(queries, keys, values, cosine, sine, chosen, w_out)


def solution(mesh):
    return jax.shard_map(
        body,
        mesh=mesh,
        in_specs=(
            P("tower", "seq", "grp"),
            P("tower", "seq", "grp"),
            P("tower", "seq", "grp"),
            P("tower", "seq"),
            P(),
            P("tower", "grp", None),
        ),
        out_specs=P("tower", "seq", "grp"),
        check_vma=False,
    )
```

```python
import functools
import math

import jax
import jax.numpy as jnp
import numpy as np
from jax import lax
from jax.experimental import pallas as pl
from jax.experimental.pallas import tpu as pltpu
from jax.sharding import PartitionSpec as P

HEAD = 128
TOK = 256
PHASES = 3
BLOCKS = 32
ROWS = 4 * TOK
MODEL = 3072
HALF = MODEL // 2
TILE = 512
SCALE = 1.0 / (math.sqrt(HEAD) * math.log(2.0))
F32 = jnp.float32
BF16 = jnp.bfloat16
MESH = pl.DeviceIdType.MESH

ALONG_X = (False, True, False)

ORDER = (
    (0, 0), (1, 0), (0, 1), (2, 0), (0, 2), (0, 3),
    (1, 1), (1, 2), (1, 3), (2, 1), (2, 2), (2, 3),
)
AHEAD = {
    ("below", 1): 8, ("above", 1): 8,
    ("below", 2): 16, ("above", 2): 16,
    ("cross", 0): 11, ("finish", 0): 15, ("project", 0): 18,
    ("cross", 1): 18, ("finish", 1): 21, ("project", 1): 22,
}
NEEDS = {
    (0, 0): ("own",), (0, 1): ("sib0",),
    (1, 0): ("below",), (1, 1): ("above",),
    (2, 0): ("sib1",), (2, 1): ("sib2",),
    (3, 0): ("opposite",), (3, 1): ("sib3",),
}


def plan():
    steps = [(phase, part, half) for phase, part in ORDER for half in range(2)]
    at = {}
    for place, (phase, part, half) in enumerate(steps):
        for event in NEEDS[(part, half)]:
            at[(event, phase)] = max(place - 1, -1)
            if event == "own":
                at[("ask", phase)] = max(place - 1, -1)
    at[("cross", 2)] = at[("sib3", 2)]
    for phase in range(PHASES):
        at[("near", phase)] = at[("sib2", phase)]
        at[("rest", phase)] = at[("sib3", phase)]
    for key, place in AHEAD.items():
        at[key] = place if key not in at else min(place, at[key])
    rank = ["ask", "own", "below", "above", "opposite", "sib0", "sib1", "sib2", "sib3",
            "near", "rest", "cross", "finish", "project"]
    slots = {}
    for (event, phase), place in sorted(at.items(), key=lambda e: (e[1], rank.index(e[0][0]), e[0][1])):
        slots.setdefault(place, []).append((event, phase))
    return slots


def pick(index, values):
    chosen = jnp.int32(values[0])
    for place in range(1, len(values)):
        chosen = jnp.where(index == place, jnp.int32(values[place]), chosen)
    return chosen


def kernel(
    q_hbm, k_hbm, v_hbm, stamps_ref, frequency_ref, partner_ref, w_hbm, out_ref,
    cos_ref, sin_ref,
    q_raw, k_raw, v_raw, w_ref, q_stage, kv_stage, kv, q_here, q_far, cross_mine, cross_far,
    held, joined, home, total, part_out, part_in,
    acc, top, block_top, scores, weights,
    load_sem, kv_s, kv_r, q_s, q_r, line_s, line_r, opp_s, opp_r, sib_s, sib_r,
    far_s, far_r, cross_s, cross_r, home_s, home_r, part_s, part_r, copy_sem,
):
    t = lax.axis_index("tower")
    c = lax.axis_index("grp")
    s = lax.axis_index("seq")
    y, x, zl = s // 8, (s // 2) % 4, s % 2
    p = zl + t - 2 * zl * t

    def place(along_x, u, w, z):
        return w * 8 + u * 2 + z if along_x else u * 8 + w * 2 + z

    class Line:
        def __init__(self, along_x):
            self.along_x = along_x
            self.u, self.w = (x, y) if along_x else (y, x)
            self.a, self.wl = self.w // 2, self.w % 2
            self.r = self.wl * 2 + zl
            self.gl = self.wl * 2 + p
            self.i = 2 * self.w + zl
            self.mine = c == self.a

        def peer(self, r):
            return (t, self.a, place(self.along_x, self.u, 2 * c + r // 2, r % 2))

        def next(self, step):
            return (t, c, place(self.along_x, (self.u + step) % 4, self.w, zl))

        def chunk(self, step, core):
            return ((self.u + step) % 4) * 8 + 4 * core

    lines = {False: Line(False), True: Line(True)}
    sibling = (t, 1 - c, s)
    far = (1 - t, c, s + 1 - 2 * zl)

    def remote(src, dst, send, recv, device):
        return pltpu.make_async_remote_copy(
            src_ref=src, dst_ref=dst, send_sem=send, recv_sem=recv,
            device_id=device, device_id_type=MESH,
        )

    loads = [
        pltpu.make_async_copy(k_hbm.at[0], k_raw, load_sem.at[0]),
        pltpu.make_async_copy(v_hbm.at[0], v_raw, load_sem.at[1]),
        pltpu.make_async_copy(q_hbm.at[0], q_raw, load_sem.at[2]),
        pltpu.make_async_copy(w_hbm.at[0], w_ref, load_sem.at[3]),
    ]
    for load in loads:
        load.start()

    barrier = pltpu.get_barrier_semaphore()

    def greet(device):
        pl.semaphore_signal(barrier, inc=1, device_id=device, device_id_type=MESH)

    count = jnp.int32(6)
    for line in lines.values():
        for r in range(4):
            @pl.when(jnp.logical_not(jnp.logical_and(line.mine, line.r == r)))
            def _():
                greet(line.peer(r))
        greet(line.next(1))
        greet(line.next(3))
        count = count + 4 - jnp.where(line.mine, 1, 0)
    greet(sibling)
    greet(far)

    def turned(raw, head):
        entries = raw[:, pl.ds(pl.multiple_of(head * HEAD, HEAD), HEAD)].astype(F32)
        swapped = pltpu.roll(entries, HEAD // 2, 1)
        return (entries * cos_ref[...] + swapped * sin_ref[...]).astype(BF16)

    def deliver(phase, gl, src, dst, send, recv):
        line = lines[ALONG_X[phase]]
        r = (gl // 2) * 2 + (gl % 2 + t - 2 * (gl % 2) * t)
        here = jnp.logical_and(line.mine, line.r == r)

        @pl.when(here)
        def _():
            pltpu.make_async_copy(src, dst, recv).start()

        @pl.when(jnp.logical_not(here))
        def _():
            remote(src, dst, send, recv, line.peer(r)).start()

    def prepare_kv(phase):
        line = lines[ALONG_X[phase]]

        def one(gl, _):
            head = gl * PHASES + phase
            kv_stage[phase * 4 + gl, 0] = turned(k_raw, head)
            kv_stage[phase * 4 + gl, 1] = v_raw[:, pl.ds(pl.multiple_of(head * HEAD, HEAD), HEAD)]
            return 0

        lax.fori_loop(0, 4, one, 0)

    def send_kv(phase):
        line = lines[ALONG_X[phase]]
        for gl in range(4):
            deliver(phase, gl, kv_stage.at[phase * 4 + gl],
                    kv.at[phase * BLOCKS + line.u * 8 + line.i],
                    kv_s.at[phase * 4 + gl], kv_r.at[phase * 4 + line.r])

    def send_q(phase):
        line = lines[ALONG_X[phase]]

        def one(gl, _):
            q_stage[phase * 4 + gl] = turned(q_raw, gl * PHASES + phase)
            return 0

        lax.fori_loop(0, 4, one, 0)
        for gl in range(4):
            deliver(phase, gl, q_stage.at[phase * 4 + gl], q_here.at[phase * 4 + line.r],
                    q_s.at[phase * 4 + gl], q_r.at[phase * 4 + line.r])

    stamps = jnp.broadcast_to(stamps_ref[...].astype(F32), (HEAD, TOK)).T
    angles = stamps * frequency_ref[...]
    column = lax.broadcasted_iota(jnp.int32, (TOK, HEAD), 1)
    sine = jnp.sin(angles)
    cos_ref[...] = jnp.cos(angles)
    sin_ref[...] = jnp.where(column < HEAD // 2, -sine, sine)
    loads[0].wait()
    loads[1].wait()
    prepare_kv(0)
    pl.semaphore_wait(barrier, count)
    send_kv(0)
    loads[2].wait()
    send_q(0)
    prepare_kv(1)
    send_kv(1)
    send_q(1)
    prepare_kv(2)
    send_kv(2)
    send_q(2)

    acc[...] = jnp.zeros(acc.shape, F32)
    top[...] = jnp.full(top.shape, -1e30, F32)

    def blocks(phase, first, size):
        return kv.at[pl.ds(phase * BLOCKS + first, size)]

    def landed(dst, recv):
        remote(dst, dst, recv, recv, sibling).wait_recv()

    def to_sibling(phase, number, part):
        remote(part, part, sib_s.at[phase * 4 + number], sib_r.at[phase * 4 + number], sibling).start()

    def event(name, phase):
        line = lines[ALONG_X[phase]]
        if name == "ask":
            for r in range(4):
                landed(q_here.at[phase * 4 + r], q_r.at[phase * 4 + r])
            remote(q_here.at[pl.ds(phase * 4, 4)], q_far.at[pl.ds(phase * 4, 4)],
                   far_s.at[phase], far_r.at[phase], far).start()
        elif name == "own":
            first = line.chunk(0, c)
            for r in range(4):
                landed(kv.at[phase * BLOCKS + first + r], kv_r.at[phase * 4 + r])
            part = blocks(phase, first, 4)
            remote(part, part, line_s.at[phase * 2], line_r.at[phase * 2], line.next(1)).start()
            remote(part, part, line_s.at[phase * 2 + 1], line_r.at[phase * 2 + 1], line.next(3)).start()
            to_sibling(phase, 0, part)
        elif name == "below":
            first = line.chunk(3, c)
            part = blocks(phase, first, 4)
            landed(part, line_r.at[phase * 2])
            passed = blocks(phase, first, 2)
            remote(passed, passed, opp_s.at[phase * 2], opp_r.at[phase * 2], line.next(1)).start()
            to_sibling(phase, 1, part)
        elif name == "above":
            first = line.chunk(1, c)
            part = blocks(phase, first, 4)
            landed(part, line_r.at[phase * 2 + 1])
            passed = blocks(phase, first + 2, 2)
            remote(passed, passed, opp_s.at[phase * 2 + 1], opp_r.at[phase * 2 + 1], line.next(3)).start()
            to_sibling(phase, 2, part)
        elif name == "opposite":
            first = line.chunk(2, c)
            landed(blocks(phase, first, 2), opp_r.at[phase * 2])
            landed(blocks(phase, first + 2, 2), opp_r.at[phase * 2 + 1])
            to_sibling(phase, 3, blocks(phase, first, 4))
        elif name[:3] == "sib":
            number = int(name[3])
            step = (0, 3, 1, 2)[number]
            landed(blocks(phase, line.chunk(step, 1 - c), 4), sib_r.at[phase * 4 + number])
        elif name == "near":
            for step in (0, 1, 3):
                copy_of(phase, step).start()
        elif name == "rest":
            copy_of(phase, 2).start()
        elif name == "cross":
            cross(phase)
        elif name == "finish":
            finish(phase)
        else:
            project(phase)

    def copy_of(phase, step):
        first = lines[ALONG_X[phase]].chunk(step, 0)
        return pltpu.make_async_copy(
            blocks(phase, first, 8), held.at[pl.ds(first, 8)], copy_sem.at[step]
        )

    def cross(phase):
        line = lines[ALONG_X[phase]]
        for step in range(4):
            copy_of(phase, step).wait()
        landed(q_far.at[pl.ds(phase * 4, 4)], far_r.at[phase])

        for r in range(4):
            asked = place(line.along_x, line.u, 2 * c + r // 2, r % 2)
            inverse = jnp.int32(0)
            for k in range(BLOCKS):
                inverse = jnp.where(partner_ref[k] == asked, k, inverse)
            want = jnp.where(t == 1, partner_ref[asked], inverse)
            if line.along_x:
                want = ((want // 2) % 4) * 8 + (want // 8) * 2 + want % 2
            found = lax.dot_general(
                q_far[phase * 4 + r], held[want, 0], (((1,), (1,)), ((), ())),
                preferred_element_type=F32,
            ) * SCALE
            exponent = jnp.exp2(found - jnp.max(found, axis=1, keepdims=True))
            denominator = jnp.sum(exponent, axis=1, keepdims=True)
            numerator = jnp.dot(exponent.astype(BF16), held[want, 1], preferred_element_type=F32)
            cross_mine[phase * 4 + r] = (numerator / denominator).astype(BF16)
            remote(cross_mine.at[phase * 4 + r], cross_far.at[phase * 4 + r],
                   cross_s.at[phase * 4 + r], cross_r.at[phase * 4 + r], far).start()

    def finish(phase):
        line = lines[ALONG_X[phase]]
        for r in range(4):
            landed(cross_far.at[phase * 4 + r], cross_r.at[phase * 4 + r])
            rows = pl.ds(phase * ROWS + r * TOK, TOK)
            own = acc[rows, 0:HEAD] / acc[rows, HEAD:]
            joined[phase * 4 + r] = (own + cross_far[phase * 4 + r].astype(F32)).astype(BF16)
            here = jnp.logical_and(line.mine, line.r == r)
            src, dst = joined.at[phase * 4 + r], home.at[phase * 4 + line.gl]
            recv = home_r.at[phase * 4 + line.gl]

            @pl.when(here)
            def _():
                pltpu.make_async_copy(src, dst, recv).start()

            @pl.when(jnp.logical_not(here))
            def _():
                remote(src, dst, home_s.at[phase * 4 + r], recv, line.peer(r)).start()

    def product(phase, columns):
        left = jnp.concatenate([home[phase * 4 + gl] for gl in range(4)], axis=1)
        right = jnp.concatenate(
            [w_ref[(gl * PHASES + phase) * HEAD:(gl * PHASES + phase + 1) * HEAD, columns]
             for gl in range(4)], axis=0)
        return jnp.dot(left, right, preferred_element_type=F32)

    def home_landed(phase):
        for gl in range(4):
            landed(home.at[phase * 4 + gl], home_r.at[phase * 4 + gl])

    def project(phase):
        home_landed(phase)
        if phase == 0:
            loads[3].wait()

        def one(n, _):
            columns = pl.ds(pl.multiple_of(n * TILE, TILE), TILE)
            value = product(phase, columns)
            total[:, columns] = value if phase == 0 else total[:, columns] + value
            return 0

        lax.fori_loop(0, MODEL // TILE, one, 0)

    def qk(phase, first, slot):
        rows = pl.ds(pl.multiple_of(phase * 4, 4), 4)
        queries = q_here[rows].reshape(ROWS, HEAD)
        keys = kv[pl.ds(phase * BLOCKS + first, 4), 0].reshape(ROWS, HEAD)
        found = lax.dot_general(
            queries, keys, (((1,), (1,)), ((), ())), preferred_element_type=F32
        )
        scores[slot] = found
        most = found[:, 0:HEAD]
        for column in range(1, ROWS // HEAD):
            most = jnp.maximum(most, found[:, column * HEAD:(column + 1) * HEAD])
        block_top[slot] = jnp.broadcast_to(
            jnp.max(most, axis=1, keepdims=True) * SCALE, (ROWS, HEAD)
        )

    def absorb(phase, first, slot):
        rows = pl.ds(pl.multiple_of(phase * ROWS, ROWS), ROWS)
        old_top = top[rows, :]
        new_top = jnp.maximum(old_top, block_top[slot])
        top[rows, :] = new_top
        for column in range(ROWS // HEAD):
            columns = slice(column * HEAD, (column + 1) * HEAD)
            weights[slot, :, columns] = jnp.exp2(
                scores[slot, :, columns] * SCALE - new_top
            ).astype(BF16)
        values = kv[pl.ds(phase * BLOCKS + first, 4), 1].reshape(ROWS, HEAD)
        widened = jnp.concatenate([values, jnp.ones_like(values)], axis=1)
        added = jnp.dot(weights[slot], widened, preferred_element_type=F32)
        rescale = jnp.exp2(old_top - new_top)
        acc[rows, :] = acc[rows, :] * jnp.concatenate([rescale, rescale], axis=1) + added

    def where_is(phase, part, half):
        u = jnp.where(pick(phase, [int(f) for f in ALONG_X]) == 1, x, y)
        step = jnp.where(part == 0, 0, jnp.where(part == 3, 2, 1 if half else 3))
        other = 1 - c
        split = other if half else c
        core = jnp.where(part == 1, c, jnp.where(part == 2, other, split))
        return ((u + step) % 4) * 8 + 4 * core

    slots = plan()
    phases = [phase for phase, part in ORDER]
    parts = [part for phase, part in ORDER]

    def events_of(pair, half):
        for number in range(len(ORDER)):
            if isinstance(pair, int) and pair != number:
                continue
            todo = slots.get(2 * number + half, [])
            if todo:
                @pl.when(pair == number)
                def _(todo=todo):
                    for name, phase in todo:
                        event(name, phase)

    for name, phase in slots.get(-1, []):
        event(name, phase)
    qk(phases[0], where_is(jnp.int32(phases[0]), jnp.int32(parts[0]), 0), 0)

    def pair_step(pair, last=False):
        following = jnp.minimum(pair + 1, len(ORDER) - 1)
        phase, part = pick(pair, phases), pick(pair, parts)
        later_phase, later_part = pick(following, phases), pick(following, parts)
        events_of(pair, 0)
        qk(phase, where_is(phase, part, 1), 1)
        absorb(phase, where_is(phase, part, 0), 0)
        events_of(pair, 1)
        if not last:
            qk(later_phase, where_is(later_phase, later_part, 0), 0)
        absorb(phase, where_is(phase, part, 1), 1)
        return 0

    lax.fori_loop(0, len(ORDER) - 1, lambda pair, _: pair_step(pair), 0)
    pair_step(jnp.int32(len(ORDER) - 1), last=True)

    finish(2)
    home_landed(2)
    theirs, ours = (1 - c) * HALF, c * HALF

    def for_sibling(n, _):
        columns = pl.ds(pl.multiple_of(theirs + n * TILE, TILE), TILE)
        here = pl.ds(pl.multiple_of(n * TILE, TILE), TILE)
        part_out[:, here] = (total[:, columns] + product(2, columns)).astype(BF16)
        return 0

    lax.fori_loop(0, HALF // TILE, for_sibling, 0)
    exchange = remote(part_out, part_in, part_s, part_r, sibling)
    exchange.start()

    def for_us(n, _):
        columns = pl.ds(pl.multiple_of(ours + n * TILE, TILE), TILE)
        total[:, columns] = total[:, columns] + product(2, columns)
        return 0

    lax.fori_loop(0, HALF // TILE, for_us, 0)
    exchange.wait()

    def emit(n, _):
        columns = pl.ds(pl.multiple_of(ours + n * TILE, TILE), TILE)
        here = pl.ds(pl.multiple_of(n * TILE, TILE), TILE)
        out_ref[0, :, here] = (total[:, columns] + part_in[:, here].astype(F32)).astype(BF16)
        return 0

    lax.fori_loop(0, HALF // TILE, emit, 0)

    def sent(src, send):
        remote(src, src, send, send, sibling).wait_send()

    for phase in range(PHASES):
        line = lines[ALONG_X[phase]]
        for number in range(4):
            r = (number // 2) * 2 + (number % 2 + t - 2 * (number % 2) * t)

            @pl.when(jnp.logical_not(jnp.logical_and(line.mine, line.r == r)))
            def _():
                sent(kv_stage.at[phase * 4 + number], kv_s.at[phase * 4 + number])
                sent(q_stage.at[phase * 4 + number], q_s.at[phase * 4 + number])

            @pl.when(jnp.logical_not(jnp.logical_and(line.mine, line.r == number)))
            def _():
                sent(joined.at[phase * 4 + number], home_s.at[phase * 4 + number])

            sent(blocks(phase, 0, 4), sib_s.at[phase * 4 + number])
            sent(cross_mine.at[phase * 4 + number], cross_s.at[phase * 4 + number])
        for number in range(2):
            sent(blocks(phase, 0, 4), line_s.at[phase * 2 + number])
            sent(blocks(phase, 0, 2), opp_s.at[phase * 2 + number])
        sent(q_here.at[pl.ds(phase * 4, 4)], far_s.at[phase])


def attention(queries, keys, values, stamps, frequency, partner, w_out):
    dma = pltpu.SemaphoreType.DMA
    anywhere = pl.BlockSpec(memory_space=pl.ANY)
    vmem = pl.BlockSpec(memory_space=pltpu.VMEM)
    heads = 4 * PHASES
    per_head = pltpu.VMEM((heads, TOK, HEAD), BF16)
    return pl.pallas_call(
        kernel,
        out_shape=jax.ShapeDtypeStruct((1, TOK, HALF), BF16),
        in_specs=[anywhere, anywhere, anywhere, vmem, vmem,
                  pl.BlockSpec(memory_space=pltpu.SMEM), anywhere],
        out_specs=vmem,
        scratch_shapes=[
            pltpu.VMEM((TOK, HEAD), F32),
            pltpu.VMEM((TOK, HEAD), F32),
            pltpu.VMEM((TOK, HALF), BF16),
            pltpu.VMEM((TOK, HALF), BF16),
            pltpu.VMEM((TOK, HALF), BF16),
            pltpu.VMEM((HALF, MODEL), BF16),
            per_head,
            pltpu.VMEM((heads, 2, TOK, HEAD), BF16),
            pltpu.VMEM((PHASES * BLOCKS, 2, TOK, HEAD), BF16),
            per_head, per_head, per_head, per_head,
            pltpu.VMEM((BLOCKS, 2, TOK, HEAD), BF16),
            per_head, per_head,
            pltpu.VMEM((TOK, MODEL), F32),
            pltpu.VMEM((TOK, HALF), BF16),
            pltpu.VMEM((TOK, HALF), BF16),
            pltpu.VMEM((PHASES * ROWS, 2 * HEAD), F32),
            pltpu.VMEM((PHASES * ROWS, HEAD), F32),
            pltpu.VMEM((2, ROWS, HEAD), F32),
            pltpu.VMEM((2, ROWS, ROWS), F32),
            pltpu.VMEM((2, ROWS, ROWS), BF16),
            dma((4,)),
            dma((heads,)), dma((heads,)), dma((heads,)), dma((heads,)),
            dma((6,)), dma((6,)), dma((6,)), dma((6,)),
            dma((heads,)), dma((heads,)),
            dma((3,)), dma((3,)), dma((heads,)), dma((heads,)),
            dma((heads,)), dma((heads,)),
            dma, dma, dma((4,)),
        ],
        compiler_params=pltpu.CompilerParams(
            collective_id=0, has_side_effects=True, vmem_limit_bytes=63 * 2**20
        ),
    )(queries, keys, values, stamps, frequency, partner, w_out)


def body(queries, keys, values, stamps, partner, w_out):
    half_size = HEAD // 2
    frequency = np.exp(-math.log(10000.0) * np.arange(half_size) / half_size)
    frequency = jnp.asarray(np.concatenate([frequency, frequency])[None, :], F32)
    return attention(queries, keys, values, stamps, frequency, partner, w_out)


def solution(mesh):
    return jax.shard_map(
        body,
        mesh=mesh,
        in_specs=(
            P("tower", "seq", "grp"),
            P("tower", "seq", "grp"),
            P("tower", "seq", "grp"),
            P("tower", "seq"),
            P(),
            P("tower", "grp", None),
        ),
        out_specs=P("tower", "seq", "grp"),
        check_vma=False,
    )
```

```python
import functools
import math

import jax
import jax.numpy as jnp
import numpy as np
from jax import lax
from jax.experimental import pallas as pl
from jax.experimental.pallas import tpu as pltpu
from jax.sharding import PartitionSpec as P

HEAD = 128
TOK = 256
PHASES = 3
BLOCKS = 32
ROWS = 4 * TOK
MODEL = 3072
HALF = MODEL // 2
TILE = 512
SCALE = 1.0 / (math.sqrt(HEAD) * math.log(2.0))
F32 = jnp.float32
BF16 = jnp.bfloat16
MESH = pl.DeviceIdType.MESH

ALONG_X = (False, True, False)

ORDER = (
    (0, 0), (1, 0), (0, 1), (2, 0), (0, 2), (0, 3),
    (1, 1), (1, 2), (1, 3), (2, 1), (2, 2), (2, 3),
)
AHEAD = {
    ("below", 1): 8, ("above", 1): 8,
    ("below", 2): 16, ("above", 2): 16,
    ("cross", 0): 11, ("finish", 0): 15, ("project", 0): 18,
    ("cross", 1): 18, ("finish", 1): 21, ("project", 1): 22,
}
NEEDS = {
    (0, 0): ("own",), (0, 1): ("sib0",),
    (1, 0): ("below",), (1, 1): ("above",),
    (2, 0): ("sib1",), (2, 1): ("sib2",),
    (3, 0): ("opposite",), (3, 1): ("sib3",),
}


def plan():
    steps = [(phase, part, half) for phase, part in ORDER for half in range(2)]
    at = {}
    for place, (phase, part, half) in enumerate(steps):
        for event in NEEDS[(part, half)]:
            at[(event, phase)] = max(place - 1, -1)
            if event == "own":
                at[("ask", phase)] = max(place - 1, -1)
    at[("cross", 2)] = at[("sib3", 2)]
    for phase in range(PHASES):
        at[("near", phase)] = at[("sib2", phase)]
        at[("rest", phase)] = at[("sib3", phase)]
    for key, place in AHEAD.items():
        at[key] = place if key not in at else min(place, at[key])
    rank = ["ask", "own", "below", "above", "opposite", "sib0", "sib1", "sib2", "sib3",
            "near", "rest", "cross", "finish", "project"]
    slots = {}
    for (event, phase), place in sorted(at.items(), key=lambda e: (e[1], rank.index(e[0][0]), e[0][1])):
        slots.setdefault(place, []).append((event, phase))
    return slots


def pick(index, values):
    chosen = jnp.int32(values[0])
    for place in range(1, len(values)):
        chosen = jnp.where(index == place, jnp.int32(values[place]), chosen)
    return chosen


def kernel(
    q_hbm, k_hbm, v_hbm, stamps_ref, frequency_ref, partner_ref, w_hbm, out_ref,
    cos_ref, sin_ref,
    q_raw, k_raw, v_raw, w_ref, q_stage, kv_stage, kv, q_here, q_far, cross_mine, cross_far,
    held, joined, home, total, part_out, part_in,
    acc, top, block_top, scores, weights,
    load_sem, kv_s, kv_r, q_s, q_r, line_s, line_r, opp_s, opp_r, sib_s, sib_r,
    far_s, far_r, cross_s, cross_r, home_s, home_r, part_s, part_r, copy_sem,
):
    t = lax.axis_index("tower")
    c = lax.axis_index("grp")
    s = lax.axis_index("seq")
    y, x, zl = s // 8, (s // 2) % 4, s % 2
    p = zl + t - 2 * zl * t

    def place(along_x, u, w, z):
        return w * 8 + u * 2 + z if along_x else u * 8 + w * 2 + z

    class Line:
        def __init__(self, along_x):
            self.along_x = along_x
            self.u, self.w = (x, y) if along_x else (y, x)
            self.a, self.wl = self.w // 2, self.w % 2
            self.r = self.wl * 2 + zl
            self.gl = self.wl * 2 + p
            self.i = 2 * self.w + zl
            self.mine = c == self.a

        def peer(self, r):
            return (t, self.a, place(self.along_x, self.u, 2 * c + r // 2, r % 2))

        def next(self, step):
            return (t, c, place(self.along_x, (self.u + step) % 4, self.w, zl))

        def chunk(self, step, core):
            return ((self.u + step) % 4) * 8 + 4 * core

    lines = {False: Line(False), True: Line(True)}
    sibling = (t, 1 - c, s)
    far = (1 - t, c, s + 1 - 2 * zl)

    def remote(src, dst, send, recv, device):
        return pltpu.make_async_remote_copy(
            src_ref=src, dst_ref=dst, send_sem=send, recv_sem=recv,
            device_id=device, device_id_type=MESH,
        )

    loads = [
        pltpu.make_async_copy(k_hbm.at[0], k_raw, load_sem.at[0]),
        pltpu.make_async_copy(v_hbm.at[0], v_raw, load_sem.at[1]),
        pltpu.make_async_copy(q_hbm.at[0], q_raw, load_sem.at[2]),
        pltpu.make_async_copy(w_hbm.at[0], w_ref, load_sem.at[3]),
    ]
    for load in loads:
        load.start()

    barrier = pltpu.get_barrier_semaphore()

    def greet(device):
        pl.semaphore_signal(barrier, inc=1, device_id=device, device_id_type=MESH)

    count = jnp.int32(6)
    for line in lines.values():
        for r in range(4):
            @pl.when(jnp.logical_not(jnp.logical_and(line.mine, line.r == r)))
            def _():
                greet(line.peer(r))
        greet(line.next(1))
        greet(line.next(3))
        count = count + 4 - jnp.where(line.mine, 1, 0)
    greet(sibling)
    greet(far)

    def turned(raw, head):
        entries = raw[:, pl.ds(pl.multiple_of(head * HEAD, HEAD), HEAD)].astype(F32)
        swapped = pltpu.roll(entries, HEAD // 2, 1)
        return (entries * cos_ref[...] + swapped * sin_ref[...]).astype(BF16)

    def deliver(phase, gl, src, dst, send, recv):
        line = lines[ALONG_X[phase]]
        r = (gl // 2) * 2 + (gl % 2 + t - 2 * (gl % 2) * t)
        here = jnp.logical_and(line.mine, line.r == r)

        @pl.when(here)
        def _():
            pltpu.make_async_copy(src, dst, recv).start()

        @pl.when(jnp.logical_not(here))
        def _():
            remote(src, dst, send, recv, line.peer(r)).start()

    def prepare_kv(phase):
        line = lines[ALONG_X[phase]]

        def one(gl, _):
            head = gl * PHASES + phase
            kv_stage[phase * 4 + gl, 0] = turned(k_raw, head)
            kv_stage[phase * 4 + gl, 1] = v_raw[:, pl.ds(pl.multiple_of(head * HEAD, HEAD), HEAD)]
            return 0

        lax.fori_loop(0, 4, one, 0)

    def send_kv(phase):
        line = lines[ALONG_X[phase]]
        for gl in range(4):
            deliver(phase, gl, kv_stage.at[phase * 4 + gl],
                    kv.at[phase * BLOCKS + line.u * 8 + line.i],
                    kv_s.at[phase * 4 + gl], kv_r.at[phase * 4 + line.r])

    def send_q(phase):
        line = lines[ALONG_X[phase]]

        def one(gl, _):
            q_stage[phase * 4 + gl] = turned(q_raw, gl * PHASES + phase)
            return 0

        lax.fori_loop(0, 4, one, 0)
        for gl in range(4):
            deliver(phase, gl, q_stage.at[phase * 4 + gl], q_here.at[phase * 4 + line.r],
                    q_s.at[phase * 4 + gl], q_r.at[phase * 4 + line.r])

    stamps = jnp.broadcast_to(stamps_ref[...].astype(F32), (HEAD, TOK)).T
    angles = stamps * frequency_ref[...]
    column = lax.broadcasted_iota(jnp.int32, (TOK, HEAD), 1)
    sine = jnp.sin(angles)
    cos_ref[...] = jnp.cos(angles)
    sin_ref[...] = jnp.where(column < HEAD // 2, -sine, sine)
    loads[0].wait()
    loads[1].wait()
    prepare_kv(0)
    pl.semaphore_wait(barrier, count)
    send_kv(0)
    loads[2].wait()
    send_q(0)
    prepare_kv(1)
    send_kv(1)
    prepare_kv(2)
    send_kv(2)
    send_q(1)
    send_q(2)

    acc[...] = jnp.zeros(acc.shape, F32)
    top[...] = jnp.full(top.shape, -1e30, F32)

    def blocks(phase, first, size):
        return kv.at[pl.ds(phase * BLOCKS + first, size)]

    def landed(dst, recv):
        remote(dst, dst, recv, recv, sibling).wait_recv()

    def to_sibling(phase, number, part):
        remote(part, part, sib_s.at[phase * 4 + number], sib_r.at[phase * 4 + number], sibling).start()

    def event(name, phase):
        line = lines[ALONG_X[phase]]
        if name == "ask":
            for r in range(4):
                landed(q_here.at[phase * 4 + r], q_r.at[phase * 4 + r])
            remote(q_here.at[pl.ds(phase * 4, 4)], q_far.at[pl.ds(phase * 4, 4)],
                   far_s.at[phase], far_r.at[phase], far).start()
        elif name == "own":
            first = line.chunk(0, c)
            for r in range(4):
                landed(kv.at[phase * BLOCKS + first + r], kv_r.at[phase * 4 + r])
            part = blocks(phase, first, 4)
            remote(part, part, line_s.at[phase * 2], line_r.at[phase * 2], line.next(1)).start()
            remote(part, part, line_s.at[phase * 2 + 1], line_r.at[phase * 2 + 1], line.next(3)).start()
            to_sibling(phase, 0, part)
        elif name == "below":
            first = line.chunk(3, c)
            part = blocks(phase, first, 4)
            landed(part, line_r.at[phase * 2])
            passed = blocks(phase, first, 2)
            remote(passed, passed, opp_s.at[phase * 2], opp_r.at[phase * 2], line.next(1)).start()
            to_sibling(phase, 1, part)
        elif name == "above":
            first = line.chunk(1, c)
            part = blocks(phase, first, 4)
            landed(part, line_r.at[phase * 2 + 1])
            passed = blocks(phase, first + 2, 2)
            remote(passed, passed, opp_s.at[phase * 2 + 1], opp_r.at[phase * 2 + 1], line.next(3)).start()
            to_sibling(phase, 2, part)
        elif name == "opposite":
            first = line.chunk(2, c)
            landed(blocks(phase, first, 2), opp_r.at[phase * 2])
            landed(blocks(phase, first + 2, 2), opp_r.at[phase * 2 + 1])
            to_sibling(phase, 3, blocks(phase, first, 4))
        elif name[:3] == "sib":
            number = int(name[3])
            step = (0, 3, 1, 2)[number]
            landed(blocks(phase, line.chunk(step, 1 - c), 4), sib_r.at[phase * 4 + number])
        elif name == "near":
            for step in (0, 1, 3):
                copy_of(phase, step).start()
        elif name == "rest":
            copy_of(phase, 2).start()
        elif name == "cross":
            cross(phase)
        elif name == "finish":
            finish(phase)
        else:
            project(phase)

    def copy_of(phase, step):
        first = lines[ALONG_X[phase]].chunk(step, 0)
        return pltpu.make_async_copy(
            blocks(phase, first, 8), held.at[pl.ds(first, 8)], copy_sem.at[step]
        )

    def cross(phase):
        line = lines[ALONG_X[phase]]
        for step in range(4):
            copy_of(phase, step).wait()
        landed(q_far.at[pl.ds(phase * 4, 4)], far_r.at[phase])

        for r in range(4):
            asked = place(line.along_x, line.u, 2 * c + r // 2, r % 2)
            inverse = jnp.int32(0)
            for k in range(BLOCKS):
                inverse = jnp.where(partner_ref[k] == asked, k, inverse)
            want = jnp.where(t == 1, partner_ref[asked], inverse)
            if line.along_x:
                want = ((want // 2) % 4) * 8 + (want // 8) * 2 + want % 2
            found = lax.dot_general(
                q_far[phase * 4 + r], held[want, 0], (((1,), (1,)), ((), ())),
                preferred_element_type=F32,
            ) * SCALE
            exponent = jnp.exp2(found - jnp.max(found, axis=1, keepdims=True))
            denominator = jnp.sum(exponent, axis=1, keepdims=True)
            numerator = jnp.dot(exponent.astype(BF16), held[want, 1], preferred_element_type=F32)
            cross_mine[phase * 4 + r] = (numerator / denominator).astype(BF16)
            remote(cross_mine.at[phase * 4 + r], cross_far.at[phase * 4 + r],
                   cross_s.at[phase * 4 + r], cross_r.at[phase * 4 + r], far).start()

    def finish(phase):
        line = lines[ALONG_X[phase]]
        for r in range(4):
            landed(cross_far.at[phase * 4 + r], cross_r.at[phase * 4 + r])
            rows = pl.ds(phase * ROWS + r * TOK, TOK)
            own = acc[rows, 0:HEAD] / acc[rows, HEAD:]
            joined[phase * 4 + r] = (own + cross_far[phase * 4 + r].astype(F32)).astype(BF16)
            here = jnp.logical_and(line.mine, line.r == r)
            src, dst = joined.at[phase * 4 + r], home.at[phase * 4 + line.gl]
            recv = home_r.at[phase * 4 + line.gl]

            @pl.when(here)
            def _():
                pltpu.make_async_copy(src, dst, recv).start()

            @pl.when(jnp.logical_not(here))
            def _():
                remote(src, dst, home_s.at[phase * 4 + r], recv, line.peer(r)).start()

    def product(phase, columns):
        left = jnp.concatenate([home[phase * 4 + gl] for gl in range(4)], axis=1)
        right = jnp.concatenate(
            [w_ref[(gl * PHASES + phase) * HEAD:(gl * PHASES + phase + 1) * HEAD, columns]
             for gl in range(4)], axis=0)
        return jnp.dot(left, right, preferred_element_type=F32)

    def home_landed(phase):
        for gl in range(4):
            landed(home.at[phase * 4 + gl], home_r.at[phase * 4 + gl])

    def project(phase):
        home_landed(phase)
        if phase == 0:
            loads[3].wait()

        def one(n, _):
            columns = pl.ds(pl.multiple_of(n * TILE, TILE), TILE)
            value = product(phase, columns)
            total[:, columns] = value if phase == 0 else total[:, columns] + value
            return 0

        lax.fori_loop(0, MODEL // TILE, one, 0)

    def qk(phase, first, slot):
        rows = pl.ds(pl.multiple_of(phase * 4, 4), 4)
        queries = q_here[rows].reshape(ROWS, HEAD)
        keys = kv[pl.ds(phase * BLOCKS + first, 4), 0].reshape(ROWS, HEAD)
        found = lax.dot_general(
            queries, keys, (((1,), (1,)), ((), ())), preferred_element_type=F32
        )
        scores[slot] = found
        most = found[:, 0:HEAD]
        for column in range(1, ROWS // HEAD):
            most = jnp.maximum(most, found[:, column * HEAD:(column + 1) * HEAD])
        block_top[slot] = jnp.broadcast_to(
            jnp.max(most, axis=1, keepdims=True) * SCALE, (ROWS, HEAD)
        )

    def absorb(phase, first, slot):
        rows = pl.ds(pl.multiple_of(phase * ROWS, ROWS), ROWS)
        old_top = top[rows, :]
        new_top = jnp.maximum(old_top, block_top[slot])
        top[rows, :] = new_top
        for column in range(ROWS // HEAD):
            columns = slice(column * HEAD, (column + 1) * HEAD)
            weights[slot, :, columns] = jnp.exp2(
                scores[slot, :, columns] * SCALE - new_top
            ).astype(BF16)
        values = kv[pl.ds(phase * BLOCKS + first, 4), 1].reshape(ROWS, HEAD)
        widened = jnp.concatenate([values, jnp.ones_like(values)], axis=1)
        added = jnp.dot(weights[slot], widened, preferred_element_type=F32)
        rescale = jnp.exp2(old_top - new_top)
        acc[rows, :] = acc[rows, :] * jnp.concatenate([rescale, rescale], axis=1) + added

    def where_is(phase, part, half):
        u = jnp.where(pick(phase, [int(f) for f in ALONG_X]) == 1, x, y)
        step = jnp.where(part == 0, 0, jnp.where(part == 3, 2, 1 if half else 3))
        other = 1 - c
        split = other if half else c
        core = jnp.where(part == 1, c, jnp.where(part == 2, other, split))
        return ((u + step) % 4) * 8 + 4 * core

    slots = plan()
    phases = [phase for phase, part in ORDER]
    parts = [part for phase, part in ORDER]

    def events_of(pair, half):
        for number in range(len(ORDER)):
            if isinstance(pair, int) and pair != number:
                continue
            todo = slots.get(2 * number + half, [])
            if todo:
                @pl.when(pair == number)
                def _(todo=todo):
                    for name, phase in todo:
                        event(name, phase)

    for name, phase in slots.get(-1, []):
        event(name, phase)
    qk(phases[0], where_is(jnp.int32(phases[0]), jnp.int32(parts[0]), 0), 0)

    def pair_step(pair, last=False):
        following = jnp.minimum(pair + 1, len(ORDER) - 1)
        phase, part = pick(pair, phases), pick(pair, parts)
        later_phase, later_part = pick(following, phases), pick(following, parts)
        events_of(pair, 0)
        qk(phase, where_is(phase, part, 1), 1)
        absorb(phase, where_is(phase, part, 0), 0)
        events_of(pair, 1)
        if not last:
            qk(later_phase, where_is(later_phase, later_part, 0), 0)
        absorb(phase, where_is(phase, part, 1), 1)
        return 0

    lax.fori_loop(0, len(ORDER) - 1, lambda pair, _: pair_step(pair), 0)
    pair_step(jnp.int32(len(ORDER) - 1), last=True)

    finish(2)
    home_landed(2)
    theirs, ours = (1 - c) * HALF, c * HALF

    def for_sibling(n, _):
        columns = pl.ds(pl.multiple_of(theirs + n * TILE, TILE), TILE)
        here = pl.ds(pl.multiple_of(n * TILE, TILE), TILE)
        part_out[:, here] = (total[:, columns] + product(2, columns)).astype(BF16)
        return 0

    lax.fori_loop(0, HALF // TILE, for_sibling, 0)
    exchange = remote(part_out, part_in, part_s, part_r, sibling)
    exchange.start()

    def for_us(n, _):
        columns = pl.ds(pl.multiple_of(ours + n * TILE, TILE), TILE)
        total[:, columns] = total[:, columns] + product(2, columns)
        return 0

    lax.fori_loop(0, HALF // TILE, for_us, 0)
    exchange.wait()

    def emit(n, _):
        columns = pl.ds(pl.multiple_of(ours + n * TILE, TILE), TILE)
        here = pl.ds(pl.multiple_of(n * TILE, TILE), TILE)
        out_ref[0, :, here] = (total[:, columns] + part_in[:, here].astype(F32)).astype(BF16)
        return 0

    lax.fori_loop(0, HALF // TILE, emit, 0)

    def sent(src, send):
        remote(src, src, send, send, sibling).wait_send()

    for phase in range(PHASES):
        line = lines[ALONG_X[phase]]
        for number in range(4):
            r = (number // 2) * 2 + (number % 2 + t - 2 * (number % 2) * t)

            @pl.when(jnp.logical_not(jnp.logical_and(line.mine, line.r == r)))
            def _():
                sent(kv_stage.at[phase * 4 + number], kv_s.at[phase * 4 + number])
                sent(q_stage.at[phase * 4 + number], q_s.at[phase * 4 + number])

            @pl.when(jnp.logical_not(jnp.logical_and(line.mine, line.r == number)))
            def _():
                sent(joined.at[phase * 4 + number], home_s.at[phase * 4 + number])

            sent(blocks(phase, 0, 4), sib_s.at[phase * 4 + number])
            sent(cross_mine.at[phase * 4 + number], cross_s.at[phase * 4 + number])
        for number in range(2):
            sent(blocks(phase, 0, 4), line_s.at[phase * 2 + number])
            sent(blocks(phase, 0, 2), opp_s.at[phase * 2 + number])
        sent(q_here.at[pl.ds(phase * 4, 4)], far_s.at[phase])


def attention(queries, keys, values, stamps, frequency, partner, w_out):
    dma = pltpu.SemaphoreType.DMA
    anywhere = pl.BlockSpec(memory_space=pl.ANY)
    vmem = pl.BlockSpec(memory_space=pltpu.VMEM)
    heads = 4 * PHASES
    per_head = pltpu.VMEM((heads, TOK, HEAD), BF16)
    return pl.pallas_call(
        kernel,
        out_shape=jax.ShapeDtypeStruct((1, TOK, HALF), BF16),
        in_specs=[anywhere, anywhere, anywhere, vmem, vmem,
                  pl.BlockSpec(memory_space=pltpu.SMEM), anywhere],
        out_specs=vmem,
        scratch_shapes=[
            pltpu.VMEM((TOK, HEAD), F32),
            pltpu.VMEM((TOK, HEAD), F32),
            pltpu.VMEM((TOK, HALF), BF16),
            pltpu.VMEM((TOK, HALF), BF16),
            pltpu.VMEM((TOK, HALF), BF16),
            pltpu.VMEM((HALF, MODEL), BF16),
            per_head,
            pltpu.VMEM((heads, 2, TOK, HEAD), BF16),
            pltpu.VMEM((PHASES * BLOCKS, 2, TOK, HEAD), BF16),
            per_head, per_head, per_head, per_head,
            pltpu.VMEM((BLOCKS, 2, TOK, HEAD), BF16),
            per_head, per_head,
            pltpu.VMEM((TOK, MODEL), F32),
            pltpu.VMEM((TOK, HALF), BF16),
            pltpu.VMEM((TOK, HALF), BF16),
            pltpu.VMEM((PHASES * ROWS, 2 * HEAD), F32),
            pltpu.VMEM((PHASES * ROWS, HEAD), F32),
            pltpu.VMEM((2, ROWS, HEAD), F32),
            pltpu.VMEM((2, ROWS, ROWS), F32),
            pltpu.VMEM((2, ROWS, ROWS), BF16),
            dma((4,)),
            dma((heads,)), dma((heads,)), dma((heads,)), dma((heads,)),
            dma((6,)), dma((6,)), dma((6,)), dma((6,)),
            dma((heads,)), dma((heads,)),
            dma((3,)), dma((3,)), dma((heads,)), dma((heads,)),
            dma((heads,)), dma((heads,)),
            dma, dma, dma((4,)),
        ],
        compiler_params=pltpu.CompilerParams(
            collective_id=0, has_side_effects=True, vmem_limit_bytes=63 * 2**20
        ),
    )(queries, keys, values, stamps, frequency, partner, w_out)


def body(queries, keys, values, stamps, partner, w_out):
    half_size = HEAD // 2
    frequency = np.exp(-math.log(10000.0) * np.arange(half_size) / half_size)
    frequency = jnp.asarray(np.concatenate([frequency, frequency])[None, :], F32)
    return attention(queries, keys, values, stamps, frequency, partner, w_out)


def solution(mesh):
    return jax.shard_map(
        body,
        mesh=mesh,
        in_specs=(
            P("tower", "seq", "grp"),
            P("tower", "seq", "grp"),
            P("tower", "seq", "grp"),
            P("tower", "seq"),
            P(),
            P("tower", "grp", None),
        ),
        out_specs=P("tower", "seq", "grp"),
        check_vma=False,
    )
```

```python
import functools
import math

import jax
import jax.numpy as jnp
import numpy as np
from jax import lax
from jax.experimental import pallas as pl
from jax.experimental.pallas import tpu as pltpu
from jax.sharding import PartitionSpec as P

HEAD = 128
TOK = 256
PHASES = 3
BLOCKS = 32
ROWS = 4 * TOK
MODEL = 3072
HALF = MODEL // 2
TILE = 512
SCALE = 1.0 / (math.sqrt(HEAD) * math.log(2.0))
F32 = jnp.float32
BF16 = jnp.bfloat16
MESH = pl.DeviceIdType.MESH

ALONG_X = (False, True, False)

ORDER = (
    (0, 0), (1, 0), (0, 1), (2, 0), (0, 2), (0, 3),
    (1, 1), (1, 2), (1, 3), (2, 1), (2, 2), (2, 3),
)
AHEAD = {
    ("kv", 1): -1, ("q", 1): -1, ("kv", 2): -1, ("q", 2): -1,
    ("below", 1): 8, ("above", 1): 8,
    ("below", 2): 16, ("above", 2): 16,
    ("cross", 0): 11, ("finish", 0): 15, ("project", 0): 18,
    ("cross", 1): 18, ("finish", 1): 21, ("project", 1): 22,
}
NEEDS = {
    (0, 0): ("own",), (0, 1): ("sib0",),
    (1, 0): ("below",), (1, 1): ("above",),
    (2, 0): ("sib1",), (2, 1): ("sib2",),
    (3, 0): ("opposite",), (3, 1): ("sib3",),
}


def plan():
    steps = [(phase, part, half) for phase, part in ORDER for half in range(2)]
    at = {}
    for place, (phase, part, half) in enumerate(steps):
        for event in NEEDS[(part, half)]:
            at[(event, phase)] = max(place - 1, -1)
            if event == "own":
                at[("ask", phase)] = max(place - 1, -1)
    at[("cross", 2)] = at[("sib3", 2)]
    for phase in range(PHASES):
        at[("near", phase)] = at[("sib2", phase)]
        at[("rest", phase)] = at[("sib3", phase)]
    for key, place in AHEAD.items():
        at[key] = place if key not in at else min(place, at[key])
    rank = ["own", "kv", "q", "ask", "below", "above", "opposite", "sib0", "sib1", "sib2", "sib3",
            "near", "rest", "cross", "finish", "project"]
    slots = {}
    for (event, phase), place in sorted(at.items(), key=lambda e: (e[1], rank.index(e[0][0]), e[0][1])):
        slots.setdefault(place, []).append((event, phase))
    return slots


def pick(index, values):
    chosen = jnp.int32(values[0])
    for place in range(1, len(values)):
        chosen = jnp.where(index == place, jnp.int32(values[place]), chosen)
    return chosen


def kernel(
    q_hbm, k_hbm, v_hbm, stamps_ref, frequency_ref, partner_ref, w_hbm, out_ref,
    cos_ref, sin_ref,
    q_raw, k_raw, v_raw, w_ref, q_stage, kv_stage, kv, q_here, q_far, cross_mine, cross_far,
    held, joined, home, total, part_out, part_in,
    acc, top, block_top, scores, weights,
    load_sem, kv_s, kv_r, q_s, q_r, line_s, line_r, opp_s, opp_r, sib_s, sib_r,
    far_s, far_r, cross_s, cross_r, home_s, home_r, part_s, part_r, copy_sem,
):
    t = lax.axis_index("tower")
    c = lax.axis_index("grp")
    s = lax.axis_index("seq")
    y, x, zl = s // 8, (s // 2) % 4, s % 2
    p = zl + t - 2 * zl * t

    def place(along_x, u, w, z):
        return w * 8 + u * 2 + z if along_x else u * 8 + w * 2 + z

    class Line:
        def __init__(self, along_x):
            self.along_x = along_x
            self.u, self.w = (x, y) if along_x else (y, x)
            self.a, self.wl = self.w // 2, self.w % 2
            self.r = self.wl * 2 + zl
            self.gl = self.wl * 2 + p
            self.i = 2 * self.w + zl
            self.mine = c == self.a

        def peer(self, r):
            return (t, self.a, place(self.along_x, self.u, 2 * c + r // 2, r % 2))

        def next(self, step):
            return (t, c, place(self.along_x, (self.u + step) % 4, self.w, zl))

        def chunk(self, step, core):
            return ((self.u + step) % 4) * 8 + 4 * core

    lines = {False: Line(False), True: Line(True)}
    sibling = (t, 1 - c, s)
    far = (1 - t, c, s + 1 - 2 * zl)

    def remote(src, dst, send, recv, device):
        return pltpu.make_async_remote_copy(
            src_ref=src, dst_ref=dst, send_sem=send, recv_sem=recv,
            device_id=device, device_id_type=MESH,
        )

    loads = [
        pltpu.make_async_copy(k_hbm.at[0], k_raw, load_sem.at[0]),
        pltpu.make_async_copy(v_hbm.at[0], v_raw, load_sem.at[1]),
        pltpu.make_async_copy(q_hbm.at[0], q_raw, load_sem.at[2]),
        pltpu.make_async_copy(w_hbm.at[0], w_ref, load_sem.at[3]),
    ]
    for load in loads:
        load.start()

    barrier = pltpu.get_barrier_semaphore()

    def greet(device):
        pl.semaphore_signal(barrier, inc=1, device_id=device, device_id_type=MESH)

    count = jnp.int32(6)
    for line in lines.values():
        for r in range(4):
            @pl.when(jnp.logical_not(jnp.logical_and(line.mine, line.r == r)))
            def _():
                greet(line.peer(r))
        greet(line.next(1))
        greet(line.next(3))
        count = count + 4 - jnp.where(line.mine, 1, 0)
    greet(sibling)
    greet(far)

    def turned(raw, head):
        entries = raw[:, pl.ds(pl.multiple_of(head * HEAD, HEAD), HEAD)].astype(F32)
        swapped = pltpu.roll(entries, HEAD // 2, 1)
        return (entries * cos_ref[...] + swapped * sin_ref[...]).astype(BF16)

    def deliver(phase, gl, src, dst, send, recv):
        line = lines[ALONG_X[phase]]
        r = (gl // 2) * 2 + (gl % 2 + t - 2 * (gl % 2) * t)
        here = jnp.logical_and(line.mine, line.r == r)

        @pl.when(here)
        def _():
            pltpu.make_async_copy(src, dst, recv).start()

        @pl.when(jnp.logical_not(here))
        def _():
            remote(src, dst, send, recv, line.peer(r)).start()

    def prepare_kv(phase):
        line = lines[ALONG_X[phase]]

        def one(gl, _):
            head = gl * PHASES + phase
            kv_stage[phase * 4 + gl, 0] = turned(k_raw, head)
            kv_stage[phase * 4 + gl, 1] = v_raw[:, pl.ds(pl.multiple_of(head * HEAD, HEAD), HEAD)]
            return 0

        lax.fori_loop(0, 4, one, 0)

    def send_kv(phase):
        line = lines[ALONG_X[phase]]
        for gl in range(4):
            deliver(phase, gl, kv_stage.at[phase * 4 + gl],
                    kv.at[phase * BLOCKS + line.u * 8 + line.i],
                    kv_s.at[phase * 4 + gl], kv_r.at[phase * 4 + line.r])

    def send_q(phase):
        line = lines[ALONG_X[phase]]

        def one(gl, _):
            q_stage[phase * 4 + gl] = turned(q_raw, gl * PHASES + phase)
            return 0

        lax.fori_loop(0, 4, one, 0)
        for gl in range(4):
            deliver(phase, gl, q_stage.at[phase * 4 + gl], q_here.at[phase * 4 + line.r],
                    q_s.at[phase * 4 + gl], q_r.at[phase * 4 + line.r])

    stamps = jnp.broadcast_to(stamps_ref[...].astype(F32), (HEAD, TOK)).T
    angles = stamps * frequency_ref[...]
    column = lax.broadcasted_iota(jnp.int32, (TOK, HEAD), 1)
    sine = jnp.sin(angles)
    cos_ref[...] = jnp.cos(angles)
    sin_ref[...] = jnp.where(column < HEAD // 2, -sine, sine)
    loads[0].wait()
    loads[1].wait()
    prepare_kv(0)
    pl.semaphore_wait(barrier, count)
    send_kv(0)
    loads[2].wait()
    send_q(0)
    prepare_kv(1)
    prepare_kv(2)

    acc[...] = jnp.zeros(acc.shape, F32)
    top[...] = jnp.full(top.shape, -1e30, F32)

    def blocks(phase, first, size):
        return kv.at[pl.ds(phase * BLOCKS + first, size)]

    def landed(dst, recv):
        remote(dst, dst, recv, recv, sibling).wait_recv()

    def to_sibling(phase, number, part):
        remote(part, part, sib_s.at[phase * 4 + number], sib_r.at[phase * 4 + number], sibling).start()

    def event(name, phase):
        line = lines[ALONG_X[phase]]
        if name == "ask":
            for r in range(4):
                landed(q_here.at[phase * 4 + r], q_r.at[phase * 4 + r])
            remote(q_here.at[pl.ds(phase * 4, 4)], q_far.at[pl.ds(phase * 4, 4)],
                   far_s.at[phase], far_r.at[phase], far).start()
        elif name == "own":
            first = line.chunk(0, c)
            for r in range(4):
                landed(kv.at[phase * BLOCKS + first + r], kv_r.at[phase * 4 + r])
            part = blocks(phase, first, 4)
            remote(part, part, line_s.at[phase * 2], line_r.at[phase * 2], line.next(1)).start()
            remote(part, part, line_s.at[phase * 2 + 1], line_r.at[phase * 2 + 1], line.next(3)).start()
            to_sibling(phase, 0, part)
        elif name == "below":
            first = line.chunk(3, c)
            part = blocks(phase, first, 4)
            landed(part, line_r.at[phase * 2])
            passed = blocks(phase, first, 2)
            remote(passed, passed, opp_s.at[phase * 2], opp_r.at[phase * 2], line.next(1)).start()
            to_sibling(phase, 1, part)
        elif name == "above":
            first = line.chunk(1, c)
            part = blocks(phase, first, 4)
            landed(part, line_r.at[phase * 2 + 1])
            passed = blocks(phase, first + 2, 2)
            remote(passed, passed, opp_s.at[phase * 2 + 1], opp_r.at[phase * 2 + 1], line.next(3)).start()
            to_sibling(phase, 2, part)
        elif name == "opposite":
            first = line.chunk(2, c)
            landed(blocks(phase, first, 2), opp_r.at[phase * 2])
            landed(blocks(phase, first + 2, 2), opp_r.at[phase * 2 + 1])
            to_sibling(phase, 3, blocks(phase, first, 4))
        elif name[:3] == "sib":
            number = int(name[3])
            step = (0, 3, 1, 2)[number]
            landed(blocks(phase, line.chunk(step, 1 - c), 4), sib_r.at[phase * 4 + number])
        elif name == "near":
            for step in (0, 1, 3):
                copy_of(phase, step).start()
        elif name == "rest":
            copy_of(phase, 2).start()
        elif name == "kv":
            send_kv(phase)
        elif name == "q":
            send_q(phase)
        elif name == "cross":
            cross(phase)
        elif name == "finish":
            finish(phase)
        else:
            project(phase)

    def copy_of(phase, step):
        first = lines[ALONG_X[phase]].chunk(step, 0)
        return pltpu.make_async_copy(
            blocks(phase, first, 8), held.at[pl.ds(first, 8)], copy_sem.at[step]
        )

    def cross(phase):
        line = lines[ALONG_X[phase]]
        for step in range(4):
            copy_of(phase, step).wait()
        landed(q_far.at[pl.ds(phase * 4, 4)], far_r.at[phase])

        for r in range(4):
            asked = place(line.along_x, line.u, 2 * c + r // 2, r % 2)
            inverse = jnp.int32(0)
            for k in range(BLOCKS):
                inverse = jnp.where(partner_ref[k] == asked, k, inverse)
            want = jnp.where(t == 1, partner_ref[asked], inverse)
            if line.along_x:
                want = ((want // 2) % 4) * 8 + (want // 8) * 2 + want % 2
            found = lax.dot_general(
                q_far[phase * 4 + r], held[want, 0], (((1,), (1,)), ((), ())),
                preferred_element_type=F32,
            ) * SCALE
            exponent = jnp.exp2(found - jnp.max(found, axis=1, keepdims=True))
            denominator = jnp.sum(exponent, axis=1, keepdims=True)
            numerator = jnp.dot(exponent.astype(BF16), held[want, 1], preferred_element_type=F32)
            cross_mine[phase * 4 + r] = (numerator / denominator).astype(BF16)
            remote(cross_mine.at[phase * 4 + r], cross_far.at[phase * 4 + r],
                   cross_s.at[phase * 4 + r], cross_r.at[phase * 4 + r], far).start()

    def finish(phase):
        line = lines[ALONG_X[phase]]
        for r in range(4):
            landed(cross_far.at[phase * 4 + r], cross_r.at[phase * 4 + r])
            rows = pl.ds(phase * ROWS + r * TOK, TOK)
            own = acc[rows, 0:HEAD] / acc[rows, HEAD:]
            joined[phase * 4 + r] = (own + cross_far[phase * 4 + r].astype(F32)).astype(BF16)
            here = jnp.logical_and(line.mine, line.r == r)
            src, dst = joined.at[phase * 4 + r], home.at[phase * 4 + line.gl]
            recv = home_r.at[phase * 4 + line.gl]

            @pl.when(here)
            def _():
                pltpu.make_async_copy(src, dst, recv).start()

            @pl.when(jnp.logical_not(here))
            def _():
                remote(src, dst, home_s.at[phase * 4 + r], recv, line.peer(r)).start()

    def product(phase, columns):
        left = jnp.concatenate([home[phase * 4 + gl] for gl in range(4)], axis=1)
        right = jnp.concatenate(
            [w_ref[(gl * PHASES + phase) * HEAD:(gl * PHASES + phase + 1) * HEAD, columns]
             for gl in range(4)], axis=0)
        return jnp.dot(left, right, preferred_element_type=F32)

    def home_landed(phase):
        for gl in range(4):
            landed(home.at[phase * 4 + gl], home_r.at[phase * 4 + gl])

    def project(phase):
        home_landed(phase)
        if phase == 0:
            loads[3].wait()

        def one(n, _):
            columns = pl.ds(pl.multiple_of(n * TILE, TILE), TILE)
            value = product(phase, columns)
            total[:, columns] = value if phase == 0 else total[:, columns] + value
            return 0

        lax.fori_loop(0, MODEL // TILE, one, 0)

    def qk(phase, first, slot):
        rows = pl.ds(pl.multiple_of(phase * 4, 4), 4)
        queries = q_here[rows].reshape(ROWS, HEAD)
        keys = kv[pl.ds(phase * BLOCKS + first, 4), 0].reshape(ROWS, HEAD)
        found = lax.dot_general(
            queries, keys, (((1,), (1,)), ((), ())), preferred_element_type=F32
        )
        scores[slot] = found
        most = found[:, 0:HEAD]
        for column in range(1, ROWS // HEAD):
            most = jnp.maximum(most, found[:, column * HEAD:(column + 1) * HEAD])
        block_top[slot] = jnp.broadcast_to(
            jnp.max(most, axis=1, keepdims=True) * SCALE, (ROWS, HEAD)
        )

    def absorb(phase, first, slot):
        rows = pl.ds(pl.multiple_of(phase * ROWS, ROWS), ROWS)
        old_top = top[rows, :]
        new_top = jnp.maximum(old_top, block_top[slot])
        top[rows, :] = new_top
        for column in range(ROWS // HEAD):
            columns = slice(column * HEAD, (column + 1) * HEAD)
            weights[slot, :, columns] = jnp.exp2(
                scores[slot, :, columns] * SCALE - new_top
            ).astype(BF16)
        values = kv[pl.ds(phase * BLOCKS + first, 4), 1].reshape(ROWS, HEAD)
        widened = jnp.concatenate([values, jnp.ones_like(values)], axis=1)
        added = jnp.dot(weights[slot], widened, preferred_element_type=F32)
        rescale = jnp.exp2(old_top - new_top)
        acc[rows, :] = acc[rows, :] * jnp.concatenate([rescale, rescale], axis=1) + added

    def where_is(phase, part, half):
        u = jnp.where(pick(phase, [int(f) for f in ALONG_X]) == 1, x, y)
        step = jnp.where(part == 0, 0, jnp.where(part == 3, 2, 1 if half else 3))
        other = 1 - c
        split = other if half else c
        core = jnp.where(part == 1, c, jnp.where(part == 2, other, split))
        return ((u + step) % 4) * 8 + 4 * core

    slots = plan()
    phases = [phase for phase, part in ORDER]
    parts = [part for phase, part in ORDER]

    def events_of(pair, half):
        for number in range(len(ORDER)):
            if isinstance(pair, int) and pair != number:
                continue
            todo = slots.get(2 * number + half, [])
            if todo:
                @pl.when(pair == number)
                def _(todo=todo):
                    for name, phase in todo:
                        event(name, phase)

    for name, phase in slots.get(-1, []):
        event(name, phase)
    qk(phases[0], where_is(jnp.int32(phases[0]), jnp.int32(parts[0]), 0), 0)

    def pair_step(pair, last=False):
        following = jnp.minimum(pair + 1, len(ORDER) - 1)
        phase, part = pick(pair, phases), pick(pair, parts)
        later_phase, later_part = pick(following, phases), pick(following, parts)
        events_of(pair, 0)
        qk(phase, where_is(phase, part, 1), 1)
        absorb(phase, where_is(phase, part, 0), 0)
        events_of(pair, 1)
        if not last:
            qk(later_phase, where_is(later_phase, later_part, 0), 0)
        absorb(phase, where_is(phase, part, 1), 1)
        return 0

    lax.fori_loop(0, len(ORDER) - 1, lambda pair, _: pair_step(pair), 0)
    pair_step(jnp.int32(len(ORDER) - 1), last=True)

    finish(2)
    home_landed(2)
    theirs, ours = (1 - c) * HALF, c * HALF

    def for_sibling(n, _):
        columns = pl.ds(pl.multiple_of(theirs + n * TILE, TILE), TILE)
        here = pl.ds(pl.multiple_of(n * TILE, TILE), TILE)
        part_out[:, here] = (total[:, columns] + product(2, columns)).astype(BF16)
        return 0

    lax.fori_loop(0, HALF // TILE, for_sibling, 0)
    exchange = remote(part_out, part_in, part_s, part_r, sibling)
    exchange.start()

    def for_us(n, _):
        columns = pl.ds(pl.multiple_of(ours + n * TILE, TILE), TILE)
        total[:, columns] = total[:, columns] + product(2, columns)
        return 0

    lax.fori_loop(0, HALF // TILE, for_us, 0)
    exchange.wait()

    def emit(n, _):
        columns = pl.ds(pl.multiple_of(ours + n * TILE, TILE), TILE)
        here = pl.ds(pl.multiple_of(n * TILE, TILE), TILE)
        out_ref[0, :, here] = (total[:, columns] + part_in[:, here].astype(F32)).astype(BF16)
        return 0

    lax.fori_loop(0, HALF // TILE, emit, 0)

    def sent(src, send):
        remote(src, src, send, send, sibling).wait_send()

    for phase in range(PHASES):
        line = lines[ALONG_X[phase]]
        for number in range(4):
            r = (number // 2) * 2 + (number % 2 + t - 2 * (number % 2) * t)

            @pl.when(jnp.logical_not(jnp.logical_and(line.mine, line.r == r)))
            def _():
                sent(kv_stage.at[phase * 4 + number], kv_s.at[phase * 4 + number])
                sent(q_stage.at[phase * 4 + number], q_s.at[phase * 4 + number])

            @pl.when(jnp.logical_not(jnp.logical_and(line.mine, line.r == number)))
            def _():
                sent(joined.at[phase * 4 + number], home_s.at[phase * 4 + number])

            sent(blocks(phase, 0, 4), sib_s.at[phase * 4 + number])
            sent(cross_mine.at[phase * 4 + number], cross_s.at[phase * 4 + number])
        for number in range(2):
            sent(blocks(phase, 0, 4), line_s.at[phase * 2 + number])
            sent(blocks(phase, 0, 2), opp_s.at[phase * 2 + number])
        sent(q_here.at[pl.ds(phase * 4, 4)], far_s.at[phase])


def attention(queries, keys, values, stamps, frequency, partner, w_out):
    dma = pltpu.SemaphoreType.DMA
    anywhere = pl.BlockSpec(memory_space=pl.ANY)
    vmem = pl.BlockSpec(memory_space=pltpu.VMEM)
    heads = 4 * PHASES
    per_head = pltpu.VMEM((heads, TOK, HEAD), BF16)
    return pl.pallas_call(
        kernel,
        out_shape=jax.ShapeDtypeStruct((1, TOK, HALF), BF16),
        in_specs=[anywhere, anywhere, anywhere, vmem, vmem,
                  pl.BlockSpec(memory_space=pltpu.SMEM), anywhere],
        out_specs=vmem,
        scratch_shapes=[
            pltpu.VMEM((TOK, HEAD), F32),
            pltpu.VMEM((TOK, HEAD), F32),
            pltpu.VMEM((TOK, HALF), BF16),
            pltpu.VMEM((TOK, HALF), BF16),
            pltpu.VMEM((TOK, HALF), BF16),
            pltpu.VMEM((HALF, MODEL), BF16),
            per_head,
            pltpu.VMEM((heads, 2, TOK, HEAD), BF16),
            pltpu.VMEM((PHASES * BLOCKS, 2, TOK, HEAD), BF16),
            per_head, per_head, per_head, per_head,
            pltpu.VMEM((BLOCKS, 2, TOK, HEAD), BF16),
            per_head, per_head,
            pltpu.VMEM((TOK, MODEL), F32),
            pltpu.VMEM((TOK, HALF), BF16),
            pltpu.VMEM((TOK, HALF), BF16),
            pltpu.VMEM((PHASES * ROWS, 2 * HEAD), F32),
            pltpu.VMEM((PHASES * ROWS, HEAD), F32),
            pltpu.VMEM((2, ROWS, HEAD), F32),
            pltpu.VMEM((2, ROWS, ROWS), F32),
            pltpu.VMEM((2, ROWS, ROWS), BF16),
            dma((4,)),
            dma((heads,)), dma((heads,)), dma((heads,)), dma((heads,)),
            dma((6,)), dma((6,)), dma((6,)), dma((6,)),
            dma((heads,)), dma((heads,)),
            dma((3,)), dma((3,)), dma((heads,)), dma((heads,)),
            dma((heads,)), dma((heads,)),
            dma, dma, dma((4,)),
        ],
        compiler_params=pltpu.CompilerParams(
            collective_id=0, has_side_effects=True, vmem_limit_bytes=63 * 2**20
        ),
    )(queries, keys, values, stamps, frequency, partner, w_out)


def body(queries, keys, values, stamps, partner, w_out):
    half_size = HEAD // 2
    frequency = np.exp(-math.log(10000.0) * np.arange(half_size) / half_size)
    frequency = jnp.asarray(np.concatenate([frequency, frequency])[None, :], F32)
    return attention(queries, keys, values, stamps, frequency, partner, w_out)


def solution(mesh):
    return jax.shard_map(
        body,
        mesh=mesh,
        in_specs=(
            P("tower", "seq", "grp"),
            P("tower", "seq", "grp"),
            P("tower", "seq", "grp"),
            P("tower", "seq"),
            P(),
            P("tower", "grp", None),
        ),
        out_specs=P("tower", "seq", "grp"),
        check_vma=False,
    )
```

```python
import functools
import math

import jax
import jax.numpy as jnp
import numpy as np
from jax import lax
from jax.experimental import pallas as pl
from jax.experimental.pallas import tpu as pltpu
from jax.sharding import PartitionSpec as P

HEAD = 128
TOK = 256
PHASES = 3
BLOCKS = 32
ROWS = 4 * TOK
MODEL = 3072
HALF = MODEL // 2
TILE = 512
SCALE = 1.0 / (math.sqrt(HEAD) * math.log(2.0))
F32 = jnp.float32
BF16 = jnp.bfloat16
MESH = pl.DeviceIdType.MESH

ALONG_X = (False, True, False)

ORDER = (
    (0, 0), (1, 0), (2, 0), (0, 1), (0, 2), (0, 3),
    (1, 1), (1, 2), (1, 3), (2, 1), (2, 2), (2, 3),
)
AHEAD = {
    ("below", 1): 8, ("above", 1): 8,
    ("below", 2): 16, ("above", 2): 16,
    ("cross", 0): 11, ("finish", 0): 15, ("project", 0): 18,
    ("cross", 1): 18, ("finish", 1): 21, ("project", 1): 22,
}
NEEDS = {
    (0, 0): ("own",), (0, 1): ("sib0",),
    (1, 0): ("below",), (1, 1): ("above",),
    (2, 0): ("sib1",), (2, 1): ("sib2",),
    (3, 0): ("opposite",), (3, 1): ("sib3",),
}


def plan():
    steps = [(phase, part, half) for phase, part in ORDER for half in range(2)]
    at = {}
    for place, (phase, part, half) in enumerate(steps):
        for event in NEEDS[(part, half)]:
            at[(event, phase)] = max(place - 1, -1)
            if event == "own":
                at[("ask", phase)] = at[("line", phase)] = max(place - 1, -1)
    at[("line", 2)] = at[("above", 0)]
    at[("cross", 2)] = at[("sib3", 2)]
    for phase in range(PHASES):
        at[("near", phase)] = at[("sib2", phase)]
        at[("rest", phase)] = at[("sib3", phase)]
    for key, place in AHEAD.items():
        at[key] = place if key not in at else min(place, at[key])
    rank = ["own", "ask", "below", "above", "line", "opposite", "sib0", "sib1", "sib2", "sib3",
            "near", "rest", "cross", "finish", "project"]
    slots = {}
    for (event, phase), place in sorted(at.items(), key=lambda e: (e[1], rank.index(e[0][0]), e[0][1])):
        slots.setdefault(place, []).append((event, phase))
    return slots


def pick(index, values):
    chosen = jnp.int32(values[0])
    for place in range(1, len(values)):
        chosen = jnp.where(index == place, jnp.int32(values[place]), chosen)
    return chosen


def kernel(
    q_hbm, k_hbm, v_hbm, stamps_ref, frequency_ref, partner_ref, w_hbm, out_ref,
    cos_ref, sin_ref,
    q_raw, k_raw, v_raw, w_ref, q_stage, kv_stage, kv, q_here, q_far, cross_mine, cross_far,
    held, joined, home, total, part_out, part_in,
    acc, top, block_top, scores, weights,
    load_sem, kv_s, kv_r, q_s, q_r, line_s, line_r, opp_s, opp_r, sib_s, sib_r,
    far_s, far_r, cross_s, cross_r, home_s, home_r, part_s, part_r, copy_sem,
):
    t = lax.axis_index("tower")
    c = lax.axis_index("grp")
    s = lax.axis_index("seq")
    y, x, zl = s // 8, (s // 2) % 4, s % 2
    p = zl + t - 2 * zl * t

    def place(along_x, u, w, z):
        return w * 8 + u * 2 + z if along_x else u * 8 + w * 2 + z

    class Line:
        def __init__(self, along_x):
            self.along_x = along_x
            self.u, self.w = (x, y) if along_x else (y, x)
            self.a, self.wl = self.w // 2, self.w % 2
            self.r = self.wl * 2 + zl
            self.gl = self.wl * 2 + p
            self.i = 2 * self.w + zl
            self.mine = c == self.a

        def peer(self, r):
            return (t, self.a, place(self.along_x, self.u, 2 * c + r // 2, r % 2))

        def next(self, step):
            return (t, c, place(self.along_x, (self.u + step) % 4, self.w, zl))

        def chunk(self, step, core):
            return ((self.u + step) % 4) * 8 + 4 * core

    lines = {False: Line(False), True: Line(True)}
    sibling = (t, 1 - c, s)
    far = (1 - t, c, s + 1 - 2 * zl)

    def remote(src, dst, send, recv, device):
        return pltpu.make_async_remote_copy(
            src_ref=src, dst_ref=dst, send_sem=send, recv_sem=recv,
            device_id=device, device_id_type=MESH,
        )

    loads = [
        pltpu.make_async_copy(k_hbm.at[0], k_raw, load_sem.at[0]),
        pltpu.make_async_copy(v_hbm.at[0], v_raw, load_sem.at[1]),
        pltpu.make_async_copy(q_hbm.at[0], q_raw, load_sem.at[2]),
        pltpu.make_async_copy(w_hbm.at[0], w_ref, load_sem.at[3]),
    ]
    for load in loads:
        load.start()

    barrier = pltpu.get_barrier_semaphore()

    def greet(device):
        pl.semaphore_signal(barrier, inc=1, device_id=device, device_id_type=MESH)

    count = jnp.int32(6)
    for line in lines.values():
        for r in range(4):
            @pl.when(jnp.logical_not(jnp.logical_and(line.mine, line.r == r)))
            def _():
                greet(line.peer(r))
        greet(line.next(1))
        greet(line.next(3))
        count = count + 4 - jnp.where(line.mine, 1, 0)
    greet(sibling)
    greet(far)

    def turned(raw, head):
        entries = raw[:, pl.ds(pl.multiple_of(head * HEAD, HEAD), HEAD)].astype(F32)
        swapped = pltpu.roll(entries, HEAD // 2, 1)
        return (entries * cos_ref[...] + swapped * sin_ref[...]).astype(BF16)

    def deliver(phase, gl, src, dst, send, recv):
        line = lines[ALONG_X[phase]]
        r = (gl // 2) * 2 + (gl % 2 + t - 2 * (gl % 2) * t)
        here = jnp.logical_and(line.mine, line.r == r)

        @pl.when(here)
        def _():
            pltpu.make_async_copy(src, dst, recv).start()

        @pl.when(jnp.logical_not(here))
        def _():
            remote(src, dst, send, recv, line.peer(r)).start()

    def prepare_kv(phase):
        line = lines[ALONG_X[phase]]

        def one(gl, _):
            head = gl * PHASES + phase
            kv_stage[phase * 4 + gl, 0] = turned(k_raw, head)
            kv_stage[phase * 4 + gl, 1] = v_raw[:, pl.ds(pl.multiple_of(head * HEAD, HEAD), HEAD)]
            return 0

        lax.fori_loop(0, 4, one, 0)

    def send_kv(phase):
        line = lines[ALONG_X[phase]]
        for gl in range(4):
            deliver(phase, gl, kv_stage.at[phase * 4 + gl],
                    kv.at[phase * BLOCKS + line.u * 8 + line.i],
                    kv_s.at[phase * 4 + gl], kv_r.at[phase * 4 + line.r])

    def send_q(phase):
        line = lines[ALONG_X[phase]]

        def one(gl, _):
            q_stage[phase * 4 + gl] = turned(q_raw, gl * PHASES + phase)
            return 0

        lax.fori_loop(0, 4, one, 0)
        for gl in range(4):
            deliver(phase, gl, q_stage.at[phase * 4 + gl], q_here.at[phase * 4 + line.r],
                    q_s.at[phase * 4 + gl], q_r.at[phase * 4 + line.r])

    stamps = jnp.broadcast_to(stamps_ref[...].astype(F32), (HEAD, TOK)).T
    angles = stamps * frequency_ref[...]
    column = lax.broadcasted_iota(jnp.int32, (TOK, HEAD), 1)
    sine = jnp.sin(angles)
    cos_ref[...] = jnp.cos(angles)
    sin_ref[...] = jnp.where(column < HEAD // 2, -sine, sine)
    loads[0].wait()
    loads[1].wait()
    prepare_kv(0)
    pl.semaphore_wait(barrier, count)
    send_kv(0)
    loads[2].wait()
    send_q(0)
    prepare_kv(1)
    send_kv(1)
    prepare_kv(2)
    send_kv(2)
    send_q(1)
    send_q(2)

    acc[...] = jnp.zeros(acc.shape, F32)
    top[...] = jnp.full(top.shape, -1e30, F32)

    def blocks(phase, first, size):
        return kv.at[pl.ds(phase * BLOCKS + first, size)]

    def landed(dst, recv):
        remote(dst, dst, recv, recv, sibling).wait_recv()

    def to_sibling(phase, number, part):
        remote(part, part, sib_s.at[phase * 4 + number], sib_r.at[phase * 4 + number], sibling).start()

    def event(name, phase):
        line = lines[ALONG_X[phase]]
        if name == "ask":
            for r in range(4):
                landed(q_here.at[phase * 4 + r], q_r.at[phase * 4 + r])
            remote(q_here.at[pl.ds(phase * 4, 4)], q_far.at[pl.ds(phase * 4, 4)],
                   far_s.at[phase], far_r.at[phase], far).start()
        elif name == "own":
            first = line.chunk(0, c)
            for r in range(4):
                landed(kv.at[phase * BLOCKS + first + r], kv_r.at[phase * 4 + r])
            to_sibling(phase, 0, blocks(phase, first, 4))
        elif name == "line":
            part = blocks(phase, line.chunk(0, c), 4)
            remote(part, part, line_s.at[phase * 2], line_r.at[phase * 2], line.next(1)).start()
            remote(part, part, line_s.at[phase * 2 + 1], line_r.at[phase * 2 + 1], line.next(3)).start()
        elif name == "below":
            first = line.chunk(3, c)
            part = blocks(phase, first, 4)
            landed(part, line_r.at[phase * 2])
            passed = blocks(phase, first, 2)
            remote(passed, passed, opp_s.at[phase * 2], opp_r.at[phase * 2], line.next(1)).start()
            to_sibling(phase, 1, part)
        elif name == "above":
            first = line.chunk(1, c)
            part = blocks(phase, first, 4)
            landed(part, line_r.at[phase * 2 + 1])
            passed = blocks(phase, first + 2, 2)
            remote(passed, passed, opp_s.at[phase * 2 + 1], opp_r.at[phase * 2 + 1], line.next(3)).start()
            to_sibling(phase, 2, part)
        elif name == "opposite":
            first = line.chunk(2, c)
            landed(blocks(phase, first, 2), opp_r.at[phase * 2])
            landed(blocks(phase, first + 2, 2), opp_r.at[phase * 2 + 1])
            to_sibling(phase, 3, blocks(phase, first, 4))
        elif name[:3] == "sib":
            number = int(name[3])
            step = (0, 3, 1, 2)[number]
            landed(blocks(phase, line.chunk(step, 1 - c), 4), sib_r.at[phase * 4 + number])
        elif name == "near":
            for step in (0, 1, 3):
                copy_of(phase, step).start()
        elif name == "rest":
            copy_of(phase, 2).start()
        elif name == "cross":
            cross(phase)
        elif name == "finish":
            finish(phase)
        else:
            project(phase)

    def copy_of(phase, step):
        first = lines[ALONG_X[phase]].chunk(step, 0)
        return pltpu.make_async_copy(
            blocks(phase, first, 8), held.at[pl.ds(first, 8)], copy_sem.at[step]
        )

    def cross(phase):
        line = lines[ALONG_X[phase]]
        for step in range(4):
            copy_of(phase, step).wait()
        landed(q_far.at[pl.ds(phase * 4, 4)], far_r.at[phase])

        for r in range(4):
            asked = place(line.along_x, line.u, 2 * c + r // 2, r % 2)
            inverse = jnp.int32(0)
            for k in range(BLOCKS):
                inverse = jnp.where(partner_ref[k] == asked, k, inverse)
            want = jnp.where(t == 1, partner_ref[asked], inverse)
            if line.along_x:
                want = ((want // 2) % 4) * 8 + (want // 8) * 2 + want % 2
            found = lax.dot_general(
                q_far[phase * 4 + r], held[want, 0], (((1,), (1,)), ((), ())),
                preferred_element_type=F32,
            ) * SCALE
            exponent = jnp.exp2(found - jnp.max(found, axis=1, keepdims=True))
            denominator = jnp.sum(exponent, axis=1, keepdims=True)
            numerator = jnp.dot(exponent.astype(BF16), held[want, 1], preferred_element_type=F32)
            cross_mine[phase * 4 + r] = (numerator / denominator).astype(BF16)
            remote(cross_mine.at[phase * 4 + r], cross_far.at[phase * 4 + r],
                   cross_s.at[phase * 4 + r], cross_r.at[phase * 4 + r], far).start()

    def finish(phase):
        line = lines[ALONG_X[phase]]
        for r in range(4):
            landed(cross_far.at[phase * 4 + r], cross_r.at[phase * 4 + r])
            rows = pl.ds(phase * ROWS + r * TOK, TOK)
            own = acc[rows, 0:HEAD] / acc[rows, HEAD:]
            joined[phase * 4 + r] = (own + cross_far[phase * 4 + r].astype(F32)).astype(BF16)
            here = jnp.logical_and(line.mine, line.r == r)
            src, dst = joined.at[phase * 4 + r], home.at[phase * 4 + line.gl]
            recv = home_r.at[phase * 4 + line.gl]

            @pl.when(here)
            def _():
                pltpu.make_async_copy(src, dst, recv).start()

            @pl.when(jnp.logical_not(here))
            def _():
                remote(src, dst, home_s.at[phase * 4 + r], recv, line.peer(r)).start()

    def product(phase, columns):
        left = jnp.concatenate([home[phase * 4 + gl] for gl in range(4)], axis=1)
        right = jnp.concatenate(
            [w_ref[(gl * PHASES + phase) * HEAD:(gl * PHASES + phase + 1) * HEAD, columns]
             for gl in range(4)], axis=0)
        return jnp.dot(left, right, preferred_element_type=F32)

    def home_landed(phase):
        for gl in range(4):
            landed(home.at[phase * 4 + gl], home_r.at[phase * 4 + gl])

    def project(phase):
        home_landed(phase)
        if phase == 0:
            loads[3].wait()

        def one(n, _):
            columns = pl.ds(pl.multiple_of(n * TILE, TILE), TILE)
            value = product(phase, columns)
            total[:, columns] = value if phase == 0 else total[:, columns] + value
            return 0

        lax.fori_loop(0, MODEL // TILE, one, 0)

    def qk(phase, first, slot):
        rows = pl.ds(pl.multiple_of(phase * 4, 4), 4)
        queries = q_here[rows].reshape(ROWS, HEAD)
        keys = kv[pl.ds(phase * BLOCKS + first, 4), 0].reshape(ROWS, HEAD)
        found = lax.dot_general(
            queries, keys, (((1,), (1,)), ((), ())), preferred_element_type=F32
        )
        scores[slot] = found
        most = found[:, 0:HEAD]
        for column in range(1, ROWS // HEAD):
            most = jnp.maximum(most, found[:, column * HEAD:(column + 1) * HEAD])
        block_top[slot] = jnp.broadcast_to(
            jnp.max(most, axis=1, keepdims=True) * SCALE, (ROWS, HEAD)
        )

    def absorb(phase, first, slot):
        rows = pl.ds(pl.multiple_of(phase * ROWS, ROWS), ROWS)
        old_top = top[rows, :]
        new_top = jnp.maximum(old_top, block_top[slot])
        top[rows, :] = new_top
        for column in range(ROWS // HEAD):
            columns = slice(column * HEAD, (column + 1) * HEAD)
            weights[slot, :, columns] = jnp.exp2(
                scores[slot, :, columns] * SCALE - new_top
            ).astype(BF16)
        values = kv[pl.ds(phase * BLOCKS + first, 4), 1].reshape(ROWS, HEAD)
        widened = jnp.concatenate([values, jnp.ones_like(values)], axis=1)
        added = jnp.dot(weights[slot], widened, preferred_element_type=F32)
        rescale = jnp.exp2(old_top - new_top)
        acc[rows, :] = acc[rows, :] * jnp.concatenate([rescale, rescale], axis=1) + added

    def where_is(phase, part, half):
        u = jnp.where(pick(phase, [int(f) for f in ALONG_X]) == 1, x, y)
        step = jnp.where(part == 0, 0, jnp.where(part == 3, 2, 1 if half else 3))
        other = 1 - c
        split = other if half else c
        core = jnp.where(part == 1, c, jnp.where(part == 2, other, split))
        return ((u + step) % 4) * 8 + 4 * core

    slots = plan()
    phases = [phase for phase, part in ORDER]
    parts = [part for phase, part in ORDER]

    def events_of(pair, half):
        for number in range(len(ORDER)):
            if isinstance(pair, int) and pair != number:
                continue
            todo = slots.get(2 * number + half, [])
            if todo:
                @pl.when(pair == number)
                def _(todo=todo):
                    for name, phase in todo:
                        event(name, phase)

    for name, phase in slots.get(-1, []):
        event(name, phase)
    qk(phases[0], where_is(jnp.int32(phases[0]), jnp.int32(parts[0]), 0), 0)

    def pair_step(pair, last=False):
        following = jnp.minimum(pair + 1, len(ORDER) - 1)
        phase, part = pick(pair, phases), pick(pair, parts)
        later_phase, later_part = pick(following, phases), pick(following, parts)
        events_of(pair, 0)
        qk(phase, where_is(phase, part, 1), 1)
        absorb(phase, where_is(phase, part, 0), 0)
        events_of(pair, 1)
        if not last:
            qk(later_phase, where_is(later_phase, later_part, 0), 0)
        absorb(phase, where_is(phase, part, 1), 1)
        return 0

    lax.fori_loop(0, len(ORDER) - 1, lambda pair, _: pair_step(pair), 0)
    pair_step(jnp.int32(len(ORDER) - 1), last=True)

    finish(2)
    home_landed(2)
    theirs, ours = (1 - c) * HALF, c * HALF

    def for_sibling(n, _):
        columns = pl.ds(pl.multiple_of(theirs + n * TILE, TILE), TILE)
        here = pl.ds(pl.multiple_of(n * TILE, TILE), TILE)
        part_out[:, here] = (total[:, columns] + product(2, columns)).astype(BF16)
        return 0

    lax.fori_loop(0, HALF // TILE, for_sibling, 0)
    exchange = remote(part_out, part_in, part_s, part_r, sibling)
    exchange.start()

    def for_us(n, _):
        columns = pl.ds(pl.multiple_of(ours + n * TILE, TILE), TILE)
        total[:, columns] = total[:, columns] + product(2, columns)
        return 0

    lax.fori_loop(0, HALF // TILE, for_us, 0)
    exchange.wait()

    def emit(n, _):
        columns = pl.ds(pl.multiple_of(ours + n * TILE, TILE), TILE)
        here = pl.ds(pl.multiple_of(n * TILE, TILE), TILE)
        out_ref[0, :, here] = (total[:, columns] + part_in[:, here].astype(F32)).astype(BF16)
        return 0

    lax.fori_loop(0, HALF // TILE, emit, 0)

    def sent(src, send):
        remote(src, src, send, send, sibling).wait_send()

    for phase in range(PHASES):
        line = lines[ALONG_X[phase]]
        for number in range(4):
            r = (number // 2) * 2 + (number % 2 + t - 2 * (number % 2) * t)

            @pl.when(jnp.logical_not(jnp.logical_and(line.mine, line.r == r)))
            def _():
                sent(kv_stage.at[phase * 4 + number], kv_s.at[phase * 4 + number])
                sent(q_stage.at[phase * 4 + number], q_s.at[phase * 4 + number])

            @pl.when(jnp.logical_not(jnp.logical_and(line.mine, line.r == number)))
            def _():
                sent(joined.at[phase * 4 + number], home_s.at[phase * 4 + number])

            sent(blocks(phase, 0, 4), sib_s.at[phase * 4 + number])
            sent(cross_mine.at[phase * 4 + number], cross_s.at[phase * 4 + number])
        for number in range(2):
            sent(blocks(phase, 0, 4), line_s.at[phase * 2 + number])
            sent(blocks(phase, 0, 2), opp_s.at[phase * 2 + number])
        sent(q_here.at[pl.ds(phase * 4, 4)], far_s.at[phase])


def attention(queries, keys, values, stamps, frequency, partner, w_out):
    dma = pltpu.SemaphoreType.DMA
    anywhere = pl.BlockSpec(memory_space=pl.ANY)
    vmem = pl.BlockSpec(memory_space=pltpu.VMEM)
    heads = 4 * PHASES
    per_head = pltpu.VMEM((heads, TOK, HEAD), BF16)
    return pl.pallas_call(
        kernel,
        out_shape=jax.ShapeDtypeStruct((1, TOK, HALF), BF16),
        in_specs=[anywhere, anywhere, anywhere, vmem, vmem,
                  pl.BlockSpec(memory_space=pltpu.SMEM), anywhere],
        out_specs=vmem,
        scratch_shapes=[
            pltpu.VMEM((TOK, HEAD), F32),
            pltpu.VMEM((TOK, HEAD), F32),
            pltpu.VMEM((TOK, HALF), BF16),
            pltpu.VMEM((TOK, HALF), BF16),
            pltpu.VMEM((TOK, HALF), BF16),
            pltpu.VMEM((HALF, MODEL), BF16),
            per_head,
            pltpu.VMEM((heads, 2, TOK, HEAD), BF16),
            pltpu.VMEM((PHASES * BLOCKS, 2, TOK, HEAD), BF16),
            per_head, per_head, per_head, per_head,
            pltpu.VMEM((BLOCKS, 2, TOK, HEAD), BF16),
            per_head, per_head,
            pltpu.VMEM((TOK, MODEL), F32),
            pltpu.VMEM((TOK, HALF), BF16),
            pltpu.VMEM((TOK, HALF), BF16),
            pltpu.VMEM((PHASES * ROWS, 2 * HEAD), F32),
            pltpu.VMEM((PHASES * ROWS, HEAD), F32),
            pltpu.VMEM((2, ROWS, HEAD), F32),
            pltpu.VMEM((2, ROWS, ROWS), F32),
            pltpu.VMEM((2, ROWS, ROWS), BF16),
            dma((4,)),
            dma((heads,)), dma((heads,)), dma((heads,)), dma((heads,)),
            dma((6,)), dma((6,)), dma((6,)), dma((6,)),
            dma((heads,)), dma((heads,)),
            dma((3,)), dma((3,)), dma((heads,)), dma((heads,)),
            dma((heads,)), dma((heads,)),
            dma, dma, dma((4,)),
        ],
        compiler_params=pltpu.CompilerParams(
            collective_id=0, has_side_effects=True, vmem_limit_bytes=63 * 2**20
        ),
    )(queries, keys, values, stamps, frequency, partner, w_out)


def body(queries, keys, values, stamps, partner, w_out):
    half_size = HEAD // 2
    frequency = np.exp(-math.log(10000.0) * np.arange(half_size) / half_size)
    frequency = jnp.asarray(np.concatenate([frequency, frequency])[None, :], F32)
    return attention(queries, keys, values, stamps, frequency, partner, w_out)


def solution(mesh):
    return jax.shard_map(
        body,
        mesh=mesh,
        in_specs=(
            P("tower", "seq", "grp"),
            P("tower", "seq", "grp"),
            P("tower", "seq", "grp"),
            P("tower", "seq"),
            P(),
            P("tower", "grp", None),
        ),
        out_specs=P("tower", "seq", "grp"),
        check_vma=False,
    )
```

```python
import functools
import math

import jax
import jax.numpy as jnp
import numpy as np
from jax import lax
from jax.experimental import pallas as pl
from jax.experimental.pallas import tpu as pltpu
from jax.sharding import PartitionSpec as P

HEAD = 128
TOK = 256
PHASES = 3
BLOCKS = 32
ROWS = 4 * TOK
MODEL = 3072
HALF = MODEL // 2
TILE = 512
SCALE = 1.0 / (math.sqrt(HEAD) * math.log(2.0))
F32 = jnp.float32
BF16 = jnp.bfloat16
MESH = pl.DeviceIdType.MESH

ALONG_X = (False, True, False)

ORDER = (
    (0, 0), (1, 0), (2, 0), (0, 1), (0, 2), (0, 3),
    (1, 1), (1, 2), (1, 3), (2, 1), (2, 2), (2, 3),
)
AHEAD = {
    ("own", 1): 0, ("line", 1): 0,
    ("below", 1): 8, ("above", 1): 8,
    ("below", 2): 16, ("above", 2): 16,
    ("cross", 0): 11, ("finish", 0): 15, ("project", 0): 18,
    ("cross", 1): 18, ("finish", 1): 21, ("project", 1): 22,
}
NEEDS = {
    (0, 0): ("own",), (0, 1): ("sib0",),
    (1, 0): ("below",), (1, 1): ("above",),
    (2, 0): ("sib1",), (2, 1): ("sib2",),
    (3, 0): ("opposite",), (3, 1): ("sib3",),
}


def plan():
    steps = [(phase, part, half) for phase, part in ORDER for half in range(2)]
    at = {}
    for place, (phase, part, half) in enumerate(steps):
        for event in NEEDS[(part, half)]:
            at[(event, phase)] = max(place - 1, -1)
            if event == "own":
                at[("ask", phase)] = at[("line", phase)] = max(place - 1, -1)
    at[("line", 2)] = at[("above", 0)]
    at[("cross", 2)] = at[("sib3", 2)]
    for phase in range(PHASES):
        at[("near", phase)] = at[("sib2", phase)]
        at[("rest", phase)] = at[("sib3", phase)]
    for key, place in AHEAD.items():
        at[key] = place if key not in at else min(place, at[key])
    rank = ["own", "line", "ask", "below", "above", "opposite", "sib0", "sib1", "sib2", "sib3",
            "near", "rest", "cross", "finish", "project"]
    slots = {}
    for (event, phase), place in sorted(at.items(), key=lambda e: (e[1], rank.index(e[0][0]), e[0][1])):
        slots.setdefault(place, []).append((event, phase))
    return slots


def pick(index, values):
    chosen = jnp.int32(values[0])
    for place in range(1, len(values)):
        chosen = jnp.where(index == place, jnp.int32(values[place]), chosen)
    return chosen


def kernel(
    q_hbm, k_hbm, v_hbm, stamps_ref, frequency_ref, partner_ref, w_hbm, out_ref,
    cos_ref, sin_ref,
    q_raw, k_raw, v_raw, w_ref, q_stage, kv_stage, kv, q_here, q_far, cross_mine, cross_far,
    held, joined, home, total, part_out, part_in,
    acc, top, block_top, scores, weights,
    load_sem, kv_s, kv_r, q_s, q_r, line_s, line_r, opp_s, opp_r, sib_s, sib_r,
    far_s, far_r, cross_s, cross_r, home_s, home_r, part_s, part_r, copy_sem,
):
    t = lax.axis_index("tower")
    c = lax.axis_index("grp")
    s = lax.axis_index("seq")
    y, x, zl = s // 8, (s // 2) % 4, s % 2
    p = zl + t - 2 * zl * t

    def place(along_x, u, w, z):
        return w * 8 + u * 2 + z if along_x else u * 8 + w * 2 + z

    class Line:
        def __init__(self, along_x):
            self.along_x = along_x
            self.u, self.w = (x, y) if along_x else (y, x)
            self.a, self.wl = self.w // 2, self.w % 2
            self.r = self.wl * 2 + zl
            self.gl = self.wl * 2 + p
            self.i = 2 * self.w + zl
            self.mine = c == self.a

        def peer(self, r):
            return (t, self.a, place(self.along_x, self.u, 2 * c + r // 2, r % 2))

        def next(self, step):
            return (t, c, place(self.along_x, (self.u + step) % 4, self.w, zl))

        def chunk(self, step, core):
            return ((self.u + step) % 4) * 8 + 4 * core

    lines = {False: Line(False), True: Line(True)}
    sibling = (t, 1 - c, s)
    far = (1 - t, c, s + 1 - 2 * zl)

    def remote(src, dst, send, recv, device):
        return pltpu.make_async_remote_copy(
            src_ref=src, dst_ref=dst, send_sem=send, recv_sem=recv,
            device_id=device, device_id_type=MESH,
        )

    loads = [
        pltpu.make_async_copy(k_hbm.at[0], k_raw, load_sem.at[0]),
        pltpu.make_async_copy(v_hbm.at[0], v_raw, load_sem.at[1]),
        pltpu.make_async_copy(q_hbm.at[0], q_raw, load_sem.at[2]),
        pltpu.make_async_copy(w_hbm.at[0], w_ref, load_sem.at[3]),
    ]
    for load in loads:
        load.start()

    barrier = pltpu.get_barrier_semaphore()

    def greet(device):
        pl.semaphore_signal(barrier, inc=1, device_id=device, device_id_type=MESH)

    count = jnp.int32(6)
    for line in lines.values():
        for r in range(4):
            @pl.when(jnp.logical_not(jnp.logical_and(line.mine, line.r == r)))
            def _():
                greet(line.peer(r))
        greet(line.next(1))
        greet(line.next(3))
        count = count + 4 - jnp.where(line.mine, 1, 0)
    greet(sibling)
    greet(far)

    def turned(raw, head):
        entries = raw[:, pl.ds(pl.multiple_of(head * HEAD, HEAD), HEAD)].astype(F32)
        swapped = pltpu.roll(entries, HEAD // 2, 1)
        return (entries * cos_ref[...] + swapped * sin_ref[...]).astype(BF16)

    def deliver(phase, gl, src, dst, send, recv):
        line = lines[ALONG_X[phase]]
        r = (gl // 2) * 2 + (gl % 2 + t - 2 * (gl % 2) * t)
        here = jnp.logical_and(line.mine, line.r == r)

        @pl.when(here)
        def _():
            pltpu.make_async_copy(src, dst, recv).start()

        @pl.when(jnp.logical_not(here))
        def _():
            remote(src, dst, send, recv, line.peer(r)).start()

    def prepare_kv(phase):
        line = lines[ALONG_X[phase]]

        def one(gl, _):
            head = gl * PHASES + phase
            kv_stage[phase * 4 + gl, 0] = turned(k_raw, head)
            kv_stage[phase * 4 + gl, 1] = v_raw[:, pl.ds(pl.multiple_of(head * HEAD, HEAD), HEAD)]
            return 0

        lax.fori_loop(0, 4, one, 0)

    def send_kv(phase):
        line = lines[ALONG_X[phase]]
        for gl in range(4):
            deliver(phase, gl, kv_stage.at[phase * 4 + gl],
                    kv.at[phase * BLOCKS + line.u * 8 + line.i],
                    kv_s.at[phase * 4 + gl], kv_r.at[phase * 4 + line.r])

    def send_q(phase):
        line = lines[ALONG_X[phase]]

        def one(gl, _):
            q_stage[phase * 4 + gl] = turned(q_raw, gl * PHASES + phase)
            return 0

        lax.fori_loop(0, 4, one, 0)
        for gl in range(4):
            deliver(phase, gl, q_stage.at[phase * 4 + gl], q_here.at[phase * 4 + line.r],
                    q_s.at[phase * 4 + gl], q_r.at[phase * 4 + line.r])

    stamps = jnp.broadcast_to(stamps_ref[...].astype(F32), (HEAD, TOK)).T
    angles = stamps * frequency_ref[...]
    column = lax.broadcasted_iota(jnp.int32, (TOK, HEAD), 1)
    sine = jnp.sin(angles)
    cos_ref[...] = jnp.cos(angles)
    sin_ref[...] = jnp.where(column < HEAD // 2, -sine, sine)
    loads[0].wait()
    loads[1].wait()
    prepare_kv(0)
    pl.semaphore_wait(barrier, count)
    send_kv(0)
    loads[2].wait()
    send_q(0)
    prepare_kv(1)
    send_kv(1)
    prepare_kv(2)
    send_kv(2)
    send_q(1)
    send_q(2)

    acc[...] = jnp.zeros(acc.shape, F32)
    top[...] = jnp.full(top.shape, -1e30, F32)

    def blocks(phase, first, size):
        return kv.at[pl.ds(phase * BLOCKS + first, size)]

    def landed(dst, recv):
        remote(dst, dst, recv, recv, sibling).wait_recv()

    def to_sibling(phase, number, part):
        remote(part, part, sib_s.at[phase * 4 + number], sib_r.at[phase * 4 + number], sibling).start()

    def event(name, phase):
        line = lines[ALONG_X[phase]]
        if name == "ask":
            for r in range(4):
                landed(q_here.at[phase * 4 + r], q_r.at[phase * 4 + r])
            remote(q_here.at[pl.ds(phase * 4, 4)], q_far.at[pl.ds(phase * 4, 4)],
                   far_s.at[phase], far_r.at[phase], far).start()
        elif name == "own":
            first = line.chunk(0, c)
            for r in range(4):
                landed(kv.at[phase * BLOCKS + first + r], kv_r.at[phase * 4 + r])
            to_sibling(phase, 0, blocks(phase, first, 4))
        elif name == "line":
            part = blocks(phase, line.chunk(0, c), 4)
            remote(part, part, line_s.at[phase * 2], line_r.at[phase * 2], line.next(1)).start()
            remote(part, part, line_s.at[phase * 2 + 1], line_r.at[phase * 2 + 1], line.next(3)).start()
        elif name == "below":
            first = line.chunk(3, c)
            part = blocks(phase, first, 4)
            landed(part, line_r.at[phase * 2])
            passed = blocks(phase, first, 2)
            remote(passed, passed, opp_s.at[phase * 2], opp_r.at[phase * 2], line.next(1)).start()
            to_sibling(phase, 1, part)
        elif name == "above":
            first = line.chunk(1, c)
            part = blocks(phase, first, 4)
            landed(part, line_r.at[phase * 2 + 1])
            passed = blocks(phase, first + 2, 2)
            remote(passed, passed, opp_s.at[phase * 2 + 1], opp_r.at[phase * 2 + 1], line.next(3)).start()
            to_sibling(phase, 2, part)
        elif name == "opposite":
            first = line.chunk(2, c)
            landed(blocks(phase, first, 2), opp_r.at[phase * 2])
            landed(blocks(phase, first + 2, 2), opp_r.at[phase * 2 + 1])
            to_sibling(phase, 3, blocks(phase, first, 4))
        elif name[:3] == "sib":
            number = int(name[3])
            step = (0, 3, 1, 2)[number]
            landed(blocks(phase, line.chunk(step, 1 - c), 4), sib_r.at[phase * 4 + number])
        elif name == "near":
            for step in (0, 1, 3):
                copy_of(phase, step).start()
        elif name == "rest":
            copy_of(phase, 2).start()
        elif name == "cross":
            cross(phase)
        elif name == "finish":
            finish(phase)
        else:
            project(phase)

    def copy_of(phase, step):
        first = lines[ALONG_X[phase]].chunk(step, 0)
        return pltpu.make_async_copy(
            blocks(phase, first, 8), held.at[pl.ds(first, 8)], copy_sem.at[step]
        )

    def cross(phase):
        line = lines[ALONG_X[phase]]
        for step in range(4):
            copy_of(phase, step).wait()
        landed(q_far.at[pl.ds(phase * 4, 4)], far_r.at[phase])

        for r in range(4):
            asked = place(line.along_x, line.u, 2 * c + r // 2, r % 2)
            inverse = jnp.int32(0)
            for k in range(BLOCKS):
                inverse = jnp.where(partner_ref[k] == asked, k, inverse)
            want = jnp.where(t == 1, partner_ref[asked], inverse)
            if line.along_x:
                want = ((want // 2) % 4) * 8 + (want // 8) * 2 + want % 2
            found = lax.dot_general(
                q_far[phase * 4 + r], held[want, 0], (((1,), (1,)), ((), ())),
                preferred_element_type=F32,
            ) * SCALE
            exponent = jnp.exp2(found - jnp.max(found, axis=1, keepdims=True))
            denominator = jnp.sum(exponent, axis=1, keepdims=True)
            numerator = jnp.dot(exponent.astype(BF16), held[want, 1], preferred_element_type=F32)
            cross_mine[phase * 4 + r] = (numerator / denominator).astype(BF16)
            remote(cross_mine.at[phase * 4 + r], cross_far.at[phase * 4 + r],
                   cross_s.at[phase * 4 + r], cross_r.at[phase * 4 + r], far).start()

    def finish(phase):
        line = lines[ALONG_X[phase]]
        for r in range(4):
            landed(cross_far.at[phase * 4 + r], cross_r.at[phase * 4 + r])
            rows = pl.ds(phase * ROWS + r * TOK, TOK)
            own = acc[rows, 0:HEAD] / acc[rows, HEAD:]
            joined[phase * 4 + r] = (own + cross_far[phase * 4 + r].astype(F32)).astype(BF16)
            here = jnp.logical_and(line.mine, line.r == r)
            src, dst = joined.at[phase * 4 + r], home.at[phase * 4 + line.gl]
            recv = home_r.at[phase * 4 + line.gl]

            @pl.when(here)
            def _():
                pltpu.make_async_copy(src, dst, recv).start()

            @pl.when(jnp.logical_not(here))
            def _():
                remote(src, dst, home_s.at[phase * 4 + r], recv, line.peer(r)).start()

    def product(phase, columns):
        left = jnp.concatenate([home[phase * 4 + gl] for gl in range(4)], axis=1)
        right = jnp.concatenate(
            [w_ref[(gl * PHASES + phase) * HEAD:(gl * PHASES + phase + 1) * HEAD, columns]
             for gl in range(4)], axis=0)
        return jnp.dot(left, right, preferred_element_type=F32)

    def home_landed(phase):
        for gl in range(4):
            landed(home.at[phase * 4 + gl], home_r.at[phase * 4 + gl])

    def project(phase):
        home_landed(phase)
        if phase == 0:
            loads[3].wait()

        def one(n, _):
            columns = pl.ds(pl.multiple_of(n * TILE, TILE), TILE)
            value = product(phase, columns)
            total[:, columns] = value if phase == 0 else total[:, columns] + value
            return 0

        lax.fori_loop(0, MODEL // TILE, one, 0)

    def qk(phase, first, slot):
        rows = pl.ds(pl.multiple_of(phase * 4, 4), 4)
        queries = q_here[rows].reshape(ROWS, HEAD)
        keys = kv[pl.ds(phase * BLOCKS + first, 4), 0].reshape(ROWS, HEAD)
        found = lax.dot_general(
            queries, keys, (((1,), (1,)), ((), ())), preferred_element_type=F32
        )
        scores[slot] = found
        most = found[:, 0:HEAD]
        for column in range(1, ROWS // HEAD):
            most = jnp.maximum(most, found[:, column * HEAD:(column + 1) * HEAD])
        block_top[slot] = jnp.broadcast_to(
            jnp.max(most, axis=1, keepdims=True) * SCALE, (ROWS, HEAD)
        )

    def absorb(phase, first, slot):
        rows = pl.ds(pl.multiple_of(phase * ROWS, ROWS), ROWS)
        old_top = top[rows, :]
        new_top = jnp.maximum(old_top, block_top[slot])
        top[rows, :] = new_top
        for column in range(ROWS // HEAD):
            columns = slice(column * HEAD, (column + 1) * HEAD)
            weights[slot, :, columns] = jnp.exp2(
                scores[slot, :, columns] * SCALE - new_top
            ).astype(BF16)
        values = kv[pl.ds(phase * BLOCKS + first, 4), 1].reshape(ROWS, HEAD)
        widened = jnp.concatenate([values, jnp.ones_like(values)], axis=1)
        added = jnp.dot(weights[slot], widened, preferred_element_type=F32)
        rescale = jnp.exp2(old_top - new_top)
        acc[rows, :] = acc[rows, :] * jnp.concatenate([rescale, rescale], axis=1) + added

    def where_is(phase, part, half):
        u = jnp.where(pick(phase, [int(f) for f in ALONG_X]) == 1, x, y)
        step = jnp.where(part == 0, 0, jnp.where(part == 3, 2, 1 if half else 3))
        other = 1 - c
        split = other if half else c
        core = jnp.where(part == 1, c, jnp.where(part == 2, other, split))
        return ((u + step) % 4) * 8 + 4 * core

    slots = plan()
    phases = [phase for phase, part in ORDER]
    parts = [part for phase, part in ORDER]

    def events_of(pair, half):
        for number in range(len(ORDER)):
            if isinstance(pair, int) and pair != number:
                continue
            todo = slots.get(2 * number + half, [])
            if todo:
                @pl.when(pair == number)
                def _(todo=todo):
                    for name, phase in todo:
                        event(name, phase)

    for name, phase in slots.get(-1, []):
        event(name, phase)
    qk(phases[0], where_is(jnp.int32(phases[0]), jnp.int32(parts[0]), 0), 0)

    def pair_step(pair, last=False):
        following = jnp.minimum(pair + 1, len(ORDER) - 1)
        phase, part = pick(pair, phases), pick(pair, parts)
        later_phase, later_part = pick(following, phases), pick(following, parts)
        events_of(pair, 0)
        qk(phase, where_is(phase, part, 1), 1)
        absorb(phase, where_is(phase, part, 0), 0)
        events_of(pair, 1)
        if not last:
            qk(later_phase, where_is(later_phase, later_part, 0), 0)
        absorb(phase, where_is(phase, part, 1), 1)
        return 0

    lax.fori_loop(0, len(ORDER) - 1, lambda pair, _: pair_step(pair), 0)
    pair_step(jnp.int32(len(ORDER) - 1), last=True)

    finish(2)
    home_landed(2)
    theirs, ours = (1 - c) * HALF, c * HALF

    exchanges = []
    for n in range(HALF // TILE):
        columns = pl.ds(pl.multiple_of(theirs + n * TILE, TILE), TILE)
        part_out[n] = (total[:, columns] + product(2, columns)).astype(BF16)
        exchanges.append(
            remote(part_out.at[n], part_in.at[n], part_s.at[n], part_r.at[n], sibling)
        )
        exchanges[-1].start()

    def for_us(n, _):
        columns = pl.ds(pl.multiple_of(ours + n * TILE, TILE), TILE)
        total[:, columns] = total[:, columns] + product(2, columns)
        return 0

    lax.fori_loop(0, HALF // TILE, for_us, 0)
    for exchange in exchanges:
        exchange.wait()

    def emit(n, _):
        columns = pl.ds(pl.multiple_of(ours + n * TILE, TILE), TILE)
        here = pl.ds(pl.multiple_of(n * TILE, TILE), TILE)
        out_ref[0, :, here] = (total[:, columns] + part_in[n].astype(F32)).astype(BF16)
        return 0

    lax.fori_loop(0, HALF // TILE, emit, 0)

    def sent(src, send):
        remote(src, src, send, send, sibling).wait_send()

    for phase in range(PHASES):
        line = lines[ALONG_X[phase]]
        for number in range(4):
            r = (number // 2) * 2 + (number % 2 + t - 2 * (number % 2) * t)

            @pl.when(jnp.logical_not(jnp.logical_and(line.mine, line.r == r)))
            def _():
                sent(kv_stage.at[phase * 4 + number], kv_s.at[phase * 4 + number])
                sent(q_stage.at[phase * 4 + number], q_s.at[phase * 4 + number])

            @pl.when(jnp.logical_not(jnp.logical_and(line.mine, line.r == number)))
            def _():
                sent(joined.at[phase * 4 + number], home_s.at[phase * 4 + number])

            sent(blocks(phase, 0, 4), sib_s.at[phase * 4 + number])
            sent(cross_mine.at[phase * 4 + number], cross_s.at[phase * 4 + number])
        for number in range(2):
            sent(blocks(phase, 0, 4), line_s.at[phase * 2 + number])
            sent(blocks(phase, 0, 2), opp_s.at[phase * 2 + number])
        sent(q_here.at[pl.ds(phase * 4, 4)], far_s.at[phase])


def attention(queries, keys, values, stamps, frequency, partner, w_out):
    dma = pltpu.SemaphoreType.DMA
    anywhere = pl.BlockSpec(memory_space=pl.ANY)
    vmem = pl.BlockSpec(memory_space=pltpu.VMEM)
    heads = 4 * PHASES
    per_head = pltpu.VMEM((heads, TOK, HEAD), BF16)
    return pl.pallas_call(
        kernel,
        out_shape=jax.ShapeDtypeStruct((1, TOK, HALF), BF16),
        in_specs=[anywhere, anywhere, anywhere, vmem, vmem,
                  pl.BlockSpec(memory_space=pltpu.SMEM), anywhere],
        out_specs=vmem,
        scratch_shapes=[
            pltpu.VMEM((TOK, HEAD), F32),
            pltpu.VMEM((TOK, HEAD), F32),
            pltpu.VMEM((TOK, HALF), BF16),
            pltpu.VMEM((TOK, HALF), BF16),
            pltpu.VMEM((TOK, HALF), BF16),
            pltpu.VMEM((HALF, MODEL), BF16),
            per_head,
            pltpu.VMEM((heads, 2, TOK, HEAD), BF16),
            pltpu.VMEM((PHASES * BLOCKS, 2, TOK, HEAD), BF16),
            per_head, per_head, per_head, per_head,
            pltpu.VMEM((BLOCKS, 2, TOK, HEAD), BF16),
            per_head, per_head,
            pltpu.VMEM((TOK, MODEL), F32),
            pltpu.VMEM((HALF // TILE, TOK, TILE), BF16),
            pltpu.VMEM((HALF // TILE, TOK, TILE), BF16),
            pltpu.VMEM((PHASES * ROWS, 2 * HEAD), F32),
            pltpu.VMEM((PHASES * ROWS, HEAD), F32),
            pltpu.VMEM((2, ROWS, HEAD), F32),
            pltpu.VMEM((2, ROWS, ROWS), F32),
            pltpu.VMEM((2, ROWS, ROWS), BF16),
            dma((4,)),
            dma((heads,)), dma((heads,)), dma((heads,)), dma((heads,)),
            dma((6,)), dma((6,)), dma((6,)), dma((6,)),
            dma((heads,)), dma((heads,)),
            dma((3,)), dma((3,)), dma((heads,)), dma((heads,)),
            dma((heads,)), dma((heads,)),
            dma((HALF // TILE,)), dma((HALF // TILE,)), dma((4,)),
        ],
        compiler_params=pltpu.CompilerParams(
            collective_id=0, has_side_effects=True, vmem_limit_bytes=63 * 2**20
        ),
    )(queries, keys, values, stamps, frequency, partner, w_out)


def body(queries, keys, values, stamps, partner, w_out):
    half_size = HEAD // 2
    frequency = np.exp(-math.log(10000.0) * np.arange(half_size) / half_size)
    frequency = jnp.asarray(np.concatenate([frequency, frequency])[None, :], F32)
    return attention(queries, keys, values, stamps, frequency, partner, w_out)


def solution(mesh):
    return jax.shard_map(
        body,
        mesh=mesh,
        in_specs=(
            P("tower", "seq", "grp"),
            P("tower", "seq", "grp"),
            P("tower", "seq", "grp"),
            P("tower", "seq"),
            P(),
            P("tower", "grp", None),
        ),
        out_specs=P("tower", "seq", "grp"),
        check_vma=False,
    )
```

```python
import functools
import math

import jax
import jax.numpy as jnp
import numpy as np
from jax import lax
from jax.experimental import pallas as pl
from jax.experimental.pallas import tpu as pltpu
from jax.sharding import PartitionSpec as P

HEAD = 128
TOK = 256
PHASES = 3
BLOCKS = 32
ROWS = 4 * TOK
MODEL = 3072
HALF = MODEL // 2
TILE = 512
SCALE = 1.0 / (math.sqrt(HEAD) * math.log(2.0))
F32 = jnp.float32
BF16 = jnp.bfloat16
MESH = pl.DeviceIdType.MESH

ALONG_X = (False, True, False)

ORDER = (
    (0, 0), (1, 0), (2, 0), (0, 1), (0, 2), (0, 3),
    (1, 1), (1, 2), (1, 3), (2, 1), (2, 2), (2, 3),
)
AHEAD = {
    ("below", 1): 8, ("above", 1): 8,
    ("below", 2): 16, ("above", 2): 16,
    ("cross", 0): 11, ("finish", 0): 15, ("project", 0): 18,
    ("cross", 1): 18, ("finish", 1): 21, ("project", 1): 22,
}
NEEDS = {
    (0, 0): ("own",), (0, 1): ("sib0",),
    (1, 0): ("below",), (1, 1): ("above",),
    (2, 0): ("sib1",), (2, 1): ("sib2",),
    (3, 0): ("opposite",), (3, 1): ("sib3",),
}


def plan():
    steps = [(phase, part, half) for phase, part in ORDER for half in range(2)]
    at = {}
    for place, (phase, part, half) in enumerate(steps):
        for event in NEEDS[(part, half)]:
            at[(event, phase)] = max(place - 1, -1)
            if event == "own":
                at[("ask", phase)] = at[("line", phase)] = max(place - 1, -1)
    at[("line", 1)] = at[("own", 2)]
    at[("line", 2)] = at[("above", 0)]
    at[("cross", 2)] = at[("sib3", 2)]
    for phase in range(PHASES):
        at[("near", phase)] = at[("sib2", phase)]
        at[("rest", phase)] = at[("sib3", phase)]
    for key, place in AHEAD.items():
        at[key] = place if key not in at else min(place, at[key])
    rank = ["own", "ask", "below", "above", "line", "opposite", "sib0", "sib1", "sib2", "sib3",
            "near", "rest", "cross", "finish", "project"]
    slots = {}
    for (event, phase), place in sorted(at.items(), key=lambda e: (e[1], rank.index(e[0][0]), e[0][1])):
        slots.setdefault(place, []).append((event, phase))
    return slots


def pick(index, values):
    chosen = jnp.int32(values[0])
    for place in range(1, len(values)):
        chosen = jnp.where(index == place, jnp.int32(values[place]), chosen)
    return chosen


def kernel(
    q_hbm, k_hbm, v_hbm, stamps_ref, frequency_ref, partner_ref, w_hbm, out_ref,
    cos_ref, sin_ref,
    q_raw, k_raw, v_raw, w_ref, q_stage, kv_stage, kv, q_here, q_far, cross_mine, cross_far,
    held, joined, home, total, part_out, part_in,
    acc, top, block_top, scores, weights,
    load_sem, kv_s, kv_r, q_s, q_r, line_s, line_r, opp_s, opp_r, sib_s, sib_r,
    far_s, far_r, cross_s, cross_r, home_s, home_r, part_s, part_r, copy_sem,
):
    t = lax.axis_index("tower")
    c = lax.axis_index("grp")
    s = lax.axis_index("seq")
    y, x, zl = s // 8, (s // 2) % 4, s % 2
    p = zl + t - 2 * zl * t

    def place(along_x, u, w, z):
        return w * 8 + u * 2 + z if along_x else u * 8 + w * 2 + z

    class Line:
        def __init__(self, along_x):
            self.along_x = along_x
            self.u, self.w = (x, y) if along_x else (y, x)
            self.a, self.wl = self.w // 2, self.w % 2
            self.r = self.wl * 2 + zl
            self.gl = self.wl * 2 + p
            self.i = 2 * self.w + zl
            self.mine = c == self.a

        def peer(self, r):
            return (t, self.a, place(self.along_x, self.u, 2 * c + r // 2, r % 2))

        def next(self, step):
            return (t, c, place(self.along_x, (self.u + step) % 4, self.w, zl))

        def chunk(self, step, core):
            return ((self.u + step) % 4) * 8 + 4 * core

    lines = {False: Line(False), True: Line(True)}
    sibling = (t, 1 - c, s)
    far = (1 - t, c, s + 1 - 2 * zl)

    def remote(src, dst, send, recv, device):
        return pltpu.make_async_remote_copy(
            src_ref=src, dst_ref=dst, send_sem=send, recv_sem=recv,
            device_id=device, device_id_type=MESH,
        )

    loads = [
        pltpu.make_async_copy(k_hbm.at[0], k_raw, load_sem.at[0]),
        pltpu.make_async_copy(v_hbm.at[0], v_raw, load_sem.at[1]),
        pltpu.make_async_copy(q_hbm.at[0], q_raw, load_sem.at[2]),
        pltpu.make_async_copy(w_hbm.at[0], w_ref, load_sem.at[3]),
    ]
    for load in loads:
        load.start()

    barrier = pltpu.get_barrier_semaphore()

    def greet(device):
        pl.semaphore_signal(barrier, inc=1, device_id=device, device_id_type=MESH)

    count = jnp.int32(6)
    for line in lines.values():
        for r in range(4):
            @pl.when(jnp.logical_not(jnp.logical_and(line.mine, line.r == r)))
            def _():
                greet(line.peer(r))
        greet(line.next(1))
        greet(line.next(3))
        count = count + 4 - jnp.where(line.mine, 1, 0)
    greet(sibling)
    greet(far)

    def turned(raw, head):
        entries = raw[:, pl.ds(pl.multiple_of(head * HEAD, HEAD), HEAD)].astype(F32)
        swapped = pltpu.roll(entries, HEAD // 2, 1)
        return (entries * cos_ref[...] + swapped * sin_ref[...]).astype(BF16)

    def deliver(phase, gl, src, dst, send, recv):
        line = lines[ALONG_X[phase]]
        r = (gl // 2) * 2 + (gl % 2 + t - 2 * (gl % 2) * t)
        here = jnp.logical_and(line.mine, line.r == r)

        @pl.when(here)
        def _():
            pltpu.make_async_copy(src, dst, recv).start()

        @pl.when(jnp.logical_not(here))
        def _():
            remote(src, dst, send, recv, line.peer(r)).start()

    def prepare_kv(phase):
        line = lines[ALONG_X[phase]]

        def one(gl, _):
            head = gl * PHASES + phase
            kv_stage[phase * 4 + gl, 0] = turned(k_raw, head)
            kv_stage[phase * 4 + gl, 1] = v_raw[:, pl.ds(pl.multiple_of(head * HEAD, HEAD), HEAD)]
            return 0

        lax.fori_loop(0, 4, one, 0)

    def send_kv(phase):
        line = lines[ALONG_X[phase]]
        for gl in range(4):
            deliver(phase, gl, kv_stage.at[phase * 4 + gl],
                    kv.at[phase * BLOCKS + line.u * 8 + line.i],
                    kv_s.at[phase * 4 + gl], kv_r.at[phase * 4 + line.r])

    def send_q(phase):
        line = lines[ALONG_X[phase]]

        def one(gl, _):
            q_stage[phase * 4 + gl] = turned(q_raw, gl * PHASES + phase)
            return 0

        lax.fori_loop(0, 4, one, 0)
        for gl in range(4):
            deliver(phase, gl, q_stage.at[phase * 4 + gl], q_here.at[phase * 4 + line.r],
                    q_s.at[phase * 4 + gl], q_r.at[phase * 4 + line.r])

    stamps = jnp.broadcast_to(stamps_ref[...].astype(F32), (HEAD, TOK)).T
    angles = stamps * frequency_ref[...]
    column = lax.broadcasted_iota(jnp.int32, (TOK, HEAD), 1)
    sine = jnp.sin(angles)
    cos_ref[...] = jnp.cos(angles)
    sin_ref[...] = jnp.where(column < HEAD // 2, -sine, sine)
    loads[0].wait()
    loads[1].wait()
    prepare_kv(0)
    pl.semaphore_wait(barrier, count)
    send_kv(0)
    loads[2].wait()
    send_q(0)
    prepare_kv(1)
    send_kv(1)
    prepare_kv(2)
    send_kv(2)
    send_q(1)
    send_q(2)

    acc[...] = jnp.zeros(acc.shape, F32)
    top[...] = jnp.full(top.shape, -1e30, F32)

    def blocks(phase, first, size):
        return kv.at[pl.ds(phase * BLOCKS + first, size)]

    def landed(dst, recv):
        remote(dst, dst, recv, recv, sibling).wait_recv()

    def to_sibling(phase, number, part):
        remote(part, part, sib_s.at[phase * 4 + number], sib_r.at[phase * 4 + number], sibling).start()

    def event(name, phase):
        line = lines[ALONG_X[phase]]
        if name == "ask":
            for r in range(4):
                landed(q_here.at[phase * 4 + r], q_r.at[phase * 4 + r])
            remote(q_here.at[pl.ds(phase * 4, 4)], q_far.at[pl.ds(phase * 4, 4)],
                   far_s.at[phase], far_r.at[phase], far).start()
        elif name == "own":
            first = line.chunk(0, c)
            for r in range(4):
                landed(kv.at[phase * BLOCKS + first + r], kv_r.at[phase * 4 + r])
            to_sibling(phase, 0, blocks(phase, first, 4))
        elif name == "line":
            part = blocks(phase, line.chunk(0, c), 4)
            remote(part, part, line_s.at[phase * 2], line_r.at[phase * 2], line.next(1)).start()
            remote(part, part, line_s.at[phase * 2 + 1], line_r.at[phase * 2 + 1], line.next(3)).start()
        elif name == "below":
            first = line.chunk(3, c)
            part = blocks(phase, first, 4)
            landed(part, line_r.at[phase * 2])
            passed = blocks(phase, first, 2)
            remote(passed, passed, opp_s.at[phase * 2], opp_r.at[phase * 2], line.next(1)).start()
            to_sibling(phase, 1, part)
        elif name == "above":
            first = line.chunk(1, c)
            part = blocks(phase, first, 4)
            landed(part, line_r.at[phase * 2 + 1])
            passed = blocks(phase, first + 2, 2)
            remote(passed, passed, opp_s.at[phase * 2 + 1], opp_r.at[phase * 2 + 1], line.next(3)).start()
            to_sibling(phase, 2, part)
        elif name == "opposite":
            first = line.chunk(2, c)
            landed(blocks(phase, first, 2), opp_r.at[phase * 2])
            landed(blocks(phase, first + 2, 2), opp_r.at[phase * 2 + 1])
            to_sibling(phase, 3, blocks(phase, first, 4))
        elif name[:3] == "sib":
            number = int(name[3])
            step = (0, 3, 1, 2)[number]
            landed(blocks(phase, line.chunk(step, 1 - c), 4), sib_r.at[phase * 4 + number])
        elif name == "near":
            for step in (0, 1, 3):
                copy_of(phase, step).start()
        elif name == "rest":
            copy_of(phase, 2).start()
        elif name == "cross":
            cross(phase)
        elif name == "finish":
            finish(phase)
        else:
            project(phase)

    def copy_of(phase, step):
        first = lines[ALONG_X[phase]].chunk(step, 0)
        return pltpu.make_async_copy(
            blocks(phase, first, 8), held.at[pl.ds(first, 8)], copy_sem.at[step]
        )

    def cross(phase):
        line = lines[ALONG_X[phase]]
        for step in range(4):
            copy_of(phase, step).wait()
        landed(q_far.at[pl.ds(phase * 4, 4)], far_r.at[phase])

        for r in range(4):
            asked = place(line.along_x, line.u, 2 * c + r // 2, r % 2)
            inverse = jnp.int32(0)
            for k in range(BLOCKS):
                inverse = jnp.where(partner_ref[k] == asked, k, inverse)
            want = jnp.where(t == 1, partner_ref[asked], inverse)
            if line.along_x:
                want = ((want // 2) % 4) * 8 + (want // 8) * 2 + want % 2
            found = lax.dot_general(
                q_far[phase * 4 + r], held[want, 0], (((1,), (1,)), ((), ())),
                preferred_element_type=F32,
            ) * SCALE
            exponent = jnp.exp2(found - jnp.max(found, axis=1, keepdims=True))
            denominator = jnp.sum(exponent, axis=1, keepdims=True)
            numerator = jnp.dot(exponent.astype(BF16), held[want, 1], preferred_element_type=F32)
            cross_mine[phase * 4 + r] = (numerator / denominator).astype(BF16)
            remote(cross_mine.at[phase * 4 + r], cross_far.at[phase * 4 + r],
                   cross_s.at[phase * 4 + r], cross_r.at[phase * 4 + r], far).start()

    def finish(phase):
        line = lines[ALONG_X[phase]]
        for r in range(4):
            landed(cross_far.at[phase * 4 + r], cross_r.at[phase * 4 + r])
            rows = pl.ds(phase * ROWS + r * TOK, TOK)
            own = acc[rows, 0:HEAD] / acc[rows, HEAD:]
            joined[phase * 4 + r] = (own + cross_far[phase * 4 + r].astype(F32)).astype(BF16)
            here = jnp.logical_and(line.mine, line.r == r)
            src, dst = joined.at[phase * 4 + r], home.at[phase * 4 + line.gl]
            recv = home_r.at[phase * 4 + line.gl]

            @pl.when(here)
            def _():
                pltpu.make_async_copy(src, dst, recv).start()

            @pl.when(jnp.logical_not(here))
            def _():
                remote(src, dst, home_s.at[phase * 4 + r], recv, line.peer(r)).start()

    def product(phase, columns):
        left = jnp.concatenate([home[phase * 4 + gl] for gl in range(4)], axis=1)
        right = jnp.concatenate(
            [w_ref[(gl * PHASES + phase) * HEAD:(gl * PHASES + phase + 1) * HEAD, columns]
             for gl in range(4)], axis=0)
        return jnp.dot(left, right, preferred_element_type=F32)

    def home_landed(phase):
        for gl in range(4):
            landed(home.at[phase * 4 + gl], home_r.at[phase * 4 + gl])

    def project(phase):
        home_landed(phase)
        if phase == 0:
            loads[3].wait()

        def one(n, _):
            columns = pl.ds(pl.multiple_of(n * TILE, TILE), TILE)
            value = product(phase, columns)
            total[:, columns] = value if phase == 0 else total[:, columns] + value
            return 0

        lax.fori_loop(0, MODEL // TILE, one, 0)

    def qk(phase, first, slot):
        rows = pl.ds(pl.multiple_of(phase * 4, 4), 4)
        queries = q_here[rows].reshape(ROWS, HEAD)
        keys = kv[pl.ds(phase * BLOCKS + first, 4), 0].reshape(ROWS, HEAD)
        found = lax.dot_general(
            queries, keys, (((1,), (1,)), ((), ())), preferred_element_type=F32
        )
        scores[slot] = found
        most = found[:, 0:HEAD]
        for column in range(1, ROWS // HEAD):
            most = jnp.maximum(most, found[:, column * HEAD:(column + 1) * HEAD])
        block_top[slot] = jnp.broadcast_to(
            jnp.max(most, axis=1, keepdims=True) * SCALE, (ROWS, HEAD)
        )

    def absorb(phase, first, slot):
        rows = pl.ds(pl.multiple_of(phase * ROWS, ROWS), ROWS)
        old_top = top[rows, :]
        new_top = jnp.maximum(old_top, block_top[slot])
        top[rows, :] = new_top
        for column in range(ROWS // HEAD):
            columns = slice(column * HEAD, (column + 1) * HEAD)
            weights[slot, :, columns] = jnp.exp2(
                scores[slot, :, columns] * SCALE - new_top
            ).astype(BF16)
        values = kv[pl.ds(phase * BLOCKS + first, 4), 1].reshape(ROWS, HEAD)
        widened = jnp.concatenate([values, jnp.ones_like(values)], axis=1)
        added = jnp.dot(weights[slot], widened, preferred_element_type=F32)
        rescale = jnp.exp2(old_top - new_top)
        acc[rows, :] = acc[rows, :] * jnp.concatenate([rescale, rescale], axis=1) + added

    def where_is(phase, part, half):
        u = jnp.where(pick(phase, [int(f) for f in ALONG_X]) == 1, x, y)
        step = jnp.where(part == 0, 0, jnp.where(part == 3, 2, 1 if half else 3))
        other = 1 - c
        split = other if half else c
        core = jnp.where(part == 1, c, jnp.where(part == 2, other, split))
        return ((u + step) % 4) * 8 + 4 * core

    slots = plan()
    phases = [phase for phase, part in ORDER]
    parts = [part for phase, part in ORDER]

    def events_of(pair, half):
        for number in range(len(ORDER)):
            if isinstance(pair, int) and pair != number:
                continue
            todo = slots.get(2 * number + half, [])
            if todo:
                @pl.when(pair == number)
                def _(todo=todo):
                    for name, phase in todo:
                        event(name, phase)

    for name, phase in slots.get(-1, []):
        event(name, phase)
    qk(phases[0], where_is(jnp.int32(phases[0]), jnp.int32(parts[0]), 0), 0)

    def pair_step(pair, last=False):
        following = jnp.minimum(pair + 1, len(ORDER) - 1)
        phase, part = pick(pair, phases), pick(pair, parts)
        later_phase, later_part = pick(following, phases), pick(following, parts)
        events_of(pair, 0)
        qk(phase, where_is(phase, part, 1), 1)
        absorb(phase, where_is(phase, part, 0), 0)
        events_of(pair, 1)
        if not last:
            qk(later_phase, where_is(later_phase, later_part, 0), 0)
        absorb(phase, where_is(phase, part, 1), 1)
        return 0

    lax.fori_loop(0, len(ORDER) - 1, lambda pair, _: pair_step(pair), 0)
    pair_step(jnp.int32(len(ORDER) - 1), last=True)

    finish(2)
    home_landed(2)
    theirs, ours = (1 - c) * HALF, c * HALF

    exchanges = []
    for n in range(HALF // TILE):
        columns = pl.ds(pl.multiple_of(theirs + n * TILE, TILE), TILE)
        part_out[n] = (total[:, columns] + product(2, columns)).astype(BF16)
        exchanges.append(
            remote(part_out.at[n], part_in.at[n], part_s.at[n], part_r.at[n], sibling)
        )
        exchanges[-1].start()

    def for_us(n, _):
        columns = pl.ds(pl.multiple_of(ours + n * TILE, TILE), TILE)
        total[:, columns] = total[:, columns] + product(2, columns)
        return 0

    lax.fori_loop(0, HALF // TILE, for_us, 0)
    for exchange in exchanges:
        exchange.wait()

    def emit(n, _):
        columns = pl.ds(pl.multiple_of(ours + n * TILE, TILE), TILE)
        here = pl.ds(pl.multiple_of(n * TILE, TILE), TILE)
        out_ref[0, :, here] = (total[:, columns] + part_in[n].astype(F32)).astype(BF16)
        return 0

    lax.fori_loop(0, HALF // TILE, emit, 0)

    def sent(src, send):
        remote(src, src, send, send, sibling).wait_send()

    for phase in range(PHASES):
        line = lines[ALONG_X[phase]]
        for number in range(4):
            r = (number // 2) * 2 + (number % 2 + t - 2 * (number % 2) * t)

            @pl.when(jnp.logical_not(jnp.logical_and(line.mine, line.r == r)))
            def _():
                sent(kv_stage.at[phase * 4 + number], kv_s.at[phase * 4 + number])
                sent(q_stage.at[phase * 4 + number], q_s.at[phase * 4 + number])

            @pl.when(jnp.logical_not(jnp.logical_and(line.mine, line.r == number)))
            def _():
                sent(joined.at[phase * 4 + number], home_s.at[phase * 4 + number])

            sent(blocks(phase, 0, 4), sib_s.at[phase * 4 + number])
            sent(cross_mine.at[phase * 4 + number], cross_s.at[phase * 4 + number])
        for number in range(2):
            sent(blocks(phase, 0, 4), line_s.at[phase * 2 + number])
            sent(blocks(phase, 0, 2), opp_s.at[phase * 2 + number])
        sent(q_here.at[pl.ds(phase * 4, 4)], far_s.at[phase])


def attention(queries, keys, values, stamps, frequency, partner, w_out):
    dma = pltpu.SemaphoreType.DMA
    anywhere = pl.BlockSpec(memory_space=pl.ANY)
    vmem = pl.BlockSpec(memory_space=pltpu.VMEM)
    heads = 4 * PHASES
    per_head = pltpu.VMEM((heads, TOK, HEAD), BF16)
    return pl.pallas_call(
        kernel,
        out_shape=jax.ShapeDtypeStruct((1, TOK, HALF), BF16),
        in_specs=[anywhere, anywhere, anywhere, vmem, vmem,
                  pl.BlockSpec(memory_space=pltpu.SMEM), anywhere],
        out_specs=vmem,
        scratch_shapes=[
            pltpu.VMEM((TOK, HEAD), F32),
            pltpu.VMEM((TOK, HEAD), F32),
            pltpu.VMEM((TOK, HALF), BF16),
            pltpu.VMEM((TOK, HALF), BF16),
            pltpu.VMEM((TOK, HALF), BF16),
            pltpu.VMEM((HALF, MODEL), BF16),
            per_head,
            pltpu.VMEM((heads, 2, TOK, HEAD), BF16),
            pltpu.VMEM((PHASES * BLOCKS, 2, TOK, HEAD), BF16),
            per_head, per_head, per_head, per_head,
            pltpu.VMEM((BLOCKS, 2, TOK, HEAD), BF16),
            per_head, per_head,
            pltpu.VMEM((TOK, MODEL), F32),
            pltpu.VMEM((HALF // TILE, TOK, TILE), BF16),
            pltpu.VMEM((HALF // TILE, TOK, TILE), BF16),
            pltpu.VMEM((PHASES * ROWS, 2 * HEAD), F32),
            pltpu.VMEM((PHASES * ROWS, HEAD), F32),
            pltpu.VMEM((2, ROWS, HEAD), F32),
            pltpu.VMEM((2, ROWS, ROWS), F32),
            pltpu.VMEM((2, ROWS, ROWS), BF16),
            dma((4,)),
            dma((heads,)), dma((heads,)), dma((heads,)), dma((heads,)),
            dma((6,)), dma((6,)), dma((6,)), dma((6,)),
            dma((heads,)), dma((heads,)),
            dma((3,)), dma((3,)), dma((heads,)), dma((heads,)),
            dma((heads,)), dma((heads,)),
            dma((HALF // TILE,)), dma((HALF // TILE,)), dma((4,)),
        ],
        compiler_params=pltpu.CompilerParams(
            collective_id=0, has_side_effects=True, vmem_limit_bytes=63 * 2**20
        ),
    )(queries, keys, values, stamps, frequency, partner, w_out)


def body(queries, keys, values, stamps, partner, w_out):
    half_size = HEAD // 2
    frequency = np.exp(-math.log(10000.0) * np.arange(half_size) / half_size)
    frequency = jnp.asarray(np.concatenate([frequency, frequency])[None, :], F32)
    return attention(queries, keys, values, stamps, frequency, partner, w_out)


def solution(mesh):
    return jax.shard_map(
        body,
        mesh=mesh,
        in_specs=(
            P("tower", "seq", "grp"),
            P("tower", "seq", "grp"),
            P("tower", "seq", "grp"),
            P("tower", "seq"),
            P(),
            P("tower", "grp", None),
        ),
        out_specs=P("tower", "seq", "grp"),
        check_vma=False,
    )
```
